32 devices in a mesh: gx: 16 (over z, x, core), gy: 2 (over y).
Axes of the slice: x: 2, y: 2, z: 4, core: 2. Of those that a mesh axis runs over, the one named last changes fastest.
Arguments:
- trial_orbitals: bfloat16 [96, 16, 32, 256], P('gx', 'gy'), may hold values from -8 to 8
- potential: float32 [96, 16, 32], P('gx', 'gy'), may hold values from 0.1 to 10
Outputs:
- filtered_orbitals: bfloat16 [96, 16, 32, 256], P('gx', 'gy')
- upper_factor: float32 [256, 256], replicated
The draws below stay inside these ranges and needn't reach their ends.
All inputs are finite; a program needn't handle non-finite values.
Results may differ from the reference program's by a relative error of at most 0.0005.
The reference program's roundings to bfloat16 on the way count: a program that leaves them out, or rounds other values in their place, can miss the bound.
Values may be sent and summed in bfloat16 or wider, within the bound.
No kernel may reach another device: no remote copies, remote signals or barrier semaphores. Data moves between devices by JAX's collectives and lax.ppermute only.
A program may use at most 64 MiB of HBM per device.

```python
import math
import jax
import jax.numpy as jnp
from jax import lax

CX = 6
CY = 8
NZ = 32
M = 256
DEG = 3
NX = 96
NY = 16
CELLS = 49152


def draw_trial_orbitals(key, part):
    key = jax.random.fold_in(key, 11)
    first = jax.random.fold_in(key, 0)
    values = jax.random.normal(first, (NX, NY, NZ, M), jnp.float32)
    return jnp.clip(values, -8.0, 8.0).astype(jnp.bfloat16)


def block_scale(own_key, dims, cuts, least, high):
    level = 1.0
    for position, parts in cuts:
        heights = jax.random.uniform(jax.random.fold_in(jax.random.fold_in(own_key, 6), position), (parts,), jnp.float32, least / len(cuts), high / len(cuts))
        level = level * jnp.repeat(jnp.exp(heights), dims[position] // parts).reshape((-1,) + (1,) * (len(dims) - 1 - position))
    return level


def setup_inputs(seed: int = 0) -> dict:
    seeds = jax.random.split(jax.random.key(seed), 3)
    trial_orbitals = draw_trial_orbitals(jax.random.fold_in(seeds[2], 71), 0)
    potential = jnp.clip(jnp.exp(math.log(10.0) - 4.6051702 * jax.random.uniform(seeds[1], (NX, NY, NZ), jnp.float32) ** block_scale(seeds[1], (NX, NY, NZ), ((0, 16), (1, 2)), -0.2, 0.2)), 0.1, 10.0)
    return {"trial_orbitals": trial_orbitals, "potential": potential}


STENCIL_WEIGHTS = (-5369.0 / 1800.0, 12.0 / 7.0, -15.0 / 56.0, 10.0 / 189.0, -1.0 / 112.0, 2.0 / 1925.0, -1.0 / 16632.0)
stencil_reach = 6
filter_center = 11.5
filter_half = 8.5

def hamiltonian(field, along_x, along_y, potential):
    extent_x = field.shape[0]
    extent_y = field.shape[1]
    extent_z = field.shape[2]
    along_z = jnp.pad(field, ((0, 0), (0, 0), (stencil_reach, stencil_reach), (0, 0)))
    center = field.astype(jnp.float32)
    laplace = 3.0 * STENCIL_WEIGHTS[0] * center
    for offset in range(1, stencil_reach + 1):
        upper = stencil_reach + offset
        lower = stencil_reach - offset
        summed = along_x[upper:upper + extent_x].astype(jnp.float32) + along_x[lower:lower + extent_x].astype(jnp.float32)
        summed = summed + along_y[:, upper:upper + extent_y].astype(jnp.float32) + along_y[:, lower:lower + extent_y].astype(jnp.float32)
        summed = summed + along_z[:, :, upper:upper + extent_z].astype(jnp.float32) + along_z[:, :, lower:lower + extent_z].astype(jnp.float32)
        laplace = laplace + STENCIL_WEIGHTS[offset] * summed
    return potential[:, :, :, None] * center - 0.5 * laplace

def chebyshev(start, apply_operator):
    previous = start
    current = ((apply_operator(start) - filter_center * start.astype(jnp.float32)) / filter_half).astype(jnp.bfloat16)
    for degree in range(1, DEG):
        shifted = apply_operator(current) - filter_center * current.astype(jnp.float32)
        following = (2.0 * shifted / filter_half - previous.astype(jnp.float32)).astype(jnp.bfloat16)
        previous, current = (current, following)
    return current

def column_cholesky(matrix):
    order = matrix.shape[0]
    index = jnp.arange(order, dtype=jnp.int32)

    def step(column, lower):
        row_j = lax.dynamic_slice_in_dim(lower, column, 1, 0)[0]
        target = lax.dynamic_slice_in_dim(matrix, column, 1, 1)[:, 0]
        partial_sum = jnp.dot(lower, row_j, precision=lax.Precision.HIGHEST, preferred_element_type=jnp.float32)
        residual = target - partial_sum
        pivot = jnp.sqrt(jnp.sum(jnp.where(index == column, residual, jnp.float32(0.0))))
        values = jnp.where(index >= column, residual / pivot, jnp.float32(0.0))
        return lax.dynamic_update_slice_in_dim(lower, values[:, None], column, 1)
    return lax.fori_loop(0, order, step, jnp.zeros((order, order), jnp.float32))

def upper_inverse(upper):
    order = upper.shape[0]
    index = jnp.arange(order, dtype=jnp.int32)

    def step(count, result):
        row = order - 1 - count
        upper_row = lax.dynamic_slice_in_dim(upper, row, 1, 0)[0]
        pivot = jnp.sum(jnp.where(index == row, upper_row, jnp.float32(0.0)))
        off_row = jnp.where(index > row, upper_row, jnp.float32(0.0))
        carried = jnp.dot(off_row, result, precision=lax.Precision.HIGHEST, preferred_element_type=jnp.float32)
        unit = jnp.where(index == row, jnp.float32(1.0), jnp.float32(0.0))
        values = (unit - carried) / pivot
        return lax.dynamic_update_slice_in_dim(result, values[None, :], row, 0)
    return lax.fori_loop(0, order, step, jnp.zeros((order, order), jnp.float32))

def reference(trial_orbitals, potential):
    group = 32
    stacked = jnp.moveaxis(trial_orbitals.reshape(NX, NY, NZ, M // group, group), 3, 0)

    def one_group(field):

        def apply_operator(values):
            padded = jnp.pad(values, ((stencil_reach, stencil_reach), (stencil_reach, stencil_reach), (0, 0), (0, 0)))
            along_x = padded[:, stencil_reach:stencil_reach + NY]
            along_y = padded[stencil_reach:stencil_reach + NX, :]
            return hamiltonian(values, along_x, along_y, potential)
        return chebyshev(field, apply_operator)
    filtered = lax.map(one_group, stacked)
    rows = jnp.moveaxis(filtered, 0, 3).reshape(CELLS, M)
    gram_matrix = lax.dot_general(rows, rows, (((0,), (0,)), ((), ())), preferred_element_type=jnp.float32)
    lower_factor = column_cholesky(gram_matrix)
    upper_factor = lower_factor.T / jnp.sqrt(jnp.float32(CELLS))
    inverse = upper_inverse(upper_factor)
    row_blocks = rows.reshape(CELLS // (CX * CY * NZ), CX * CY * NZ, M)

    def rotate(block):
        return jnp.dot(block.astype(jnp.float32), inverse, precision=lax.Precision.HIGHEST, preferred_element_type=jnp.float32).astype(jnp.bfloat16)
    orbitals = lax.map(rotate, row_blocks)
    return (orbitals.reshape(NX, NY, NZ, M), upper_factor)
```

```python
import functools
import math

import jax
import jax.numpy as jnp
import ml_dtypes
import numpy as np
from jax import lax
from jax.experimental import pallas as pl
from jax.experimental.pallas import tpu as pltpu
from jax.sharding import PartitionSpec as P

DEG = 3


STENCIL_WEIGHTS = (
    -5369.0 / 1800.0,
    12.0 / 7.0,
    -15.0 / 56.0,
    10.0 / 189.0,
    -1.0 / 112.0,
    2.0 / 1925.0,
    -1.0 / 16632.0,
)
stencil_reach = 6
filter_center = 11.5
filter_half = 8.5
axes = ("gx", "gy")
vmem_limit = 48 * 1024 * 1024

center_shift = -1.5 * STENCIL_WEIGHTS[0] - filter_center
side_weights = tuple(-0.5 * weight / filter_half for weight in STENCIL_WEIGHTS)


def exact_parts(values):
    parts = []
    rest = np.asarray(values, np.float32)
    for _ in range(3):
        part = rest.astype(ml_dtypes.bfloat16)
        parts.append(part)
        rest = rest - part.astype(np.float32)
    return np.stack(parts)


def plane_weights(extent_y, extent_z):
    def band(extent, shift):
        matrix = np.zeros((extent, extent), np.float64)
        for source in range(extent):
            for target in range(extent):
                distance = abs(target - (source + shift))
                if 1 <= distance <= stencil_reach:
                    matrix[source, target] = side_weights[distance]
        return matrix

    eye_y, eye_z = np.eye(extent_y), np.eye(extent_z)
    own = np.kron(band(extent_y, 0), eye_z) + np.kron(eye_y, band(extent_z, 0))
    before = np.kron(band(extent_y, -extent_y), eye_z)
    after = np.kron(band(extent_y, extent_y), eye_z)
    return np.stack([exact_parts(part) for part in (own, before, after)])


def split_kernel(cells_ref, sent_ref):
    devices, rows, plane = sent_ref.shape
    layers = cells_ref.shape[0] // plane
    share = rows // layers
    for layer in range(0, layers, 2):
        pair = []
        for at in (layer, layer + 1):
            block = cells_ref[at * plane : (at + 1) * plane, :].astype(jnp.float32)
            pair.append(block.T.reshape(devices, share, plane))
        both = jnp.concatenate(pair, axis=1)
        sent_ref[:, layer * share : (layer + 2) * share, :] = both.astype(jnp.bfloat16)


def split_columns(cells, devices, plane):
    count, columns = cells.shape
    layers = count // plane
    share = columns // devices
    if share % 8 == 0 and layers % 2 == 0:
        return pl.pallas_call(
            split_kernel,
            out_shape=jax.ShapeDtypeStruct((devices, layers * share, plane), jnp.bfloat16),
            compiler_params=pltpu.CompilerParams(vmem_limit_bytes=vmem_limit),
        )(cells)
    spread = cells.reshape(layers, plane, devices, share).transpose(2, 0, 3, 1)
    return spread.reshape(devices, layers * share, plane)


def join_kernel(received_ref, cells_ref, gram_ref):
    devices, rows, plane = received_ref.shape
    layers = cells_ref.shape[0] // plane
    share = rows // layers
    columns = devices * share
    total = None
    for layer in range(0, layers, 2):
        both = received_ref[:, layer * share : (layer + 2) * share, :].astype(jnp.float32)
        for side in range(2):
            block = both[:, side * share : (side + 1) * share, :].reshape(columns, plane)
            at = (layer + side) * plane
            cells_ref[at : at + plane, :] = block.T.astype(jnp.bfloat16)
            narrow = block.astype(jnp.bfloat16)
            part = lax.dot_general(
                narrow, narrow, (((1,), (1,)), ((), ())), preferred_element_type=jnp.float32
            )
            total = part if total is None else total + part
    gram_ref[...] = total


def join_columns(received, layers):
    devices, rows, plane = received.shape
    share = rows // layers
    columns = devices * share
    if share % 8 == 0 and layers % 2 == 0:
        return pl.pallas_call(
            join_kernel,
            out_shape=(
                jax.ShapeDtypeStruct((layers * plane, columns), jnp.bfloat16),
                jax.ShapeDtypeStruct((columns, columns), jnp.float32),
            ),
            compiler_params=pltpu.CompilerParams(vmem_limit_bytes=vmem_limit),
        )(received)
    cells = received.reshape(devices, layers, share, plane).transpose(1, 3, 0, 2)
    cells = cells.reshape(layers * plane, columns)
    gram = lax.dot_general(cells, cells, (((0,), (0,)), ((), ())), preferred_element_type=jnp.float32)
    return cells, gram


def filter_kernel(
    bricks_x, bricks_y, received_ref, potential_ref, weights_ref, sent_ref,
    start_ref, first_ref, second_ref, plane_ref, center_ref,
):
    _, rows, plane = received_ref.shape
    layers = potential_ref.shape[1]
    share = rows // layers
    total = bricks_x * rows
    margin = stencil_reach * share
    for ref in (start_ref, first_ref, second_ref):
        ref[:margin, :] = jnp.zeros((margin, bricks_y * plane), jnp.float32)
        ref[margin + total :, :] = jnp.zeros((margin, bricks_y * plane), jnp.float32)
    for brick in range(bricks_x * bricks_y):
        at = margin + brick // bricks_y * rows
        lanes_at = brick % bricks_y * plane
        start_ref[at : at + rows, lanes_at : lanes_at + plane] = received_ref[brick].astype(jnp.float32)
        level = (potential_ref[brick] + center_shift) * (1.0 / filter_half)
        level = jnp.broadcast_to(level[:, None, :], (layers, share, plane)).reshape(rows, plane)
        center_ref[at - margin : at - margin + rows, lanes_at : lanes_at + plane] = level

    def apply(field_ref, write):
        narrow = [
            field_ref[margin : margin + total, b * plane : (b + 1) * plane].astype(jnp.bfloat16)
            for b in range(bricks_y)
        ]
        for b in range(bricks_y):
            fields, weights = [], []
            for kind, other in ((0, b), (1, b - 1), (2, b + 1)):
                if 0 <= other < bricks_y:
                    for part in range(weights_ref.shape[1]):
                        fields.append(narrow[other])
                        weights.append(weights_ref[kind, part])
            plane_ref[:, b * plane : (b + 1) * plane] = jnp.dot(
                jnp.concatenate(fields, axis=1),
                jnp.concatenate(weights, axis=0),
                preferred_element_type=jnp.float32,
            )

        def one_brick(brick, at):
            for b in range(bricks_y):
                here = slice(b * plane, (b + 1) * plane)
                window = field_ref[pl.ds(at, rows + 2 * margin), here]
                value = center_ref[pl.ds(at, rows), here] * window[margin : margin + rows]
                value = value + plane_ref[pl.ds(at, rows), here]
                for distance in range(1, stencil_reach + 1):
                    low = margin - distance * share
                    high = margin + distance * share
                    pair = window[low : low + rows] + window[high : high + rows]
                    value = value + side_weights[distance] * pair
                write(brick, b, at, here, value)

        if rows % 8 == 0:
            @pl.loop(0, bricks_x)
            def _(brick):
                one_brick(brick, pl.multiple_of(brick * rows, 8))
        else:
            for brick in range(bricks_x):
                one_brick(brick, brick * rows)

    def write_first(brick, b, at, here, value):
        first_ref[pl.ds(at + margin, rows), here] = value.astype(jnp.bfloat16).astype(jnp.float32)

    def write_second(brick, b, at, here, value):
        following = 2.0 * value - start_ref[pl.ds(at + margin, rows), here]
        second_ref[pl.ds(at + margin, rows), here] = following.astype(jnp.bfloat16).astype(jnp.float32)

    def write_third(brick, b, at, here, value):
        following = 2.0 * value - first_ref[pl.ds(at + margin, rows), here]
        sent_ref[brick * bricks_y + b] = following.astype(jnp.bfloat16)

    apply(start_ref, write_first)
    apply(first_ref, write_second)
    apply(second_ref, write_third)


def filter_columns(received, potential, weights, bricks_x, bricks_y):
    _, rows, plane = received.shape
    share = rows // potential.shape[1]
    total = bricks_x * rows
    padded = total + 2 * stencil_reach * share
    width = bricks_y * plane
    field = pltpu.VMEM((padded, width), jnp.float32)
    whole = pltpu.VMEM((total, width), jnp.float32)
    return pl.pallas_call(
        functools.partial(filter_kernel, bricks_x, bricks_y),
        out_shape=jax.ShapeDtypeStruct(received.shape, jnp.bfloat16),
        scratch_shapes=[field, field, field, whole, whole],
        compiler_params=pltpu.CompilerParams(vmem_limit_bytes=vmem_limit),
    )(received, potential, weights)


lanes = 128
panel_rows = 8
block_rows = 64


def row_splat(values, row):
    return jnp.broadcast_to(values[row : row + 1, :], values.shape)


def lane_splat(values, lane):
    return jnp.broadcast_to(values[:, lane : lane + 1], (panel_rows, lanes))


def panel_inverse(columns):
    row = lax.broadcasted_iota(jnp.int32, (panel_rows, lanes), 0)
    columns = list(columns)
    full = [jnp.where(row == k, 1.0, 0.0).astype(jnp.float32) for k in range(panel_rows)]
    forward = list(full)
    pivots = jnp.zeros((panel_rows, lanes), jnp.float32)
    for step in range(panel_rows):
        pivot = row_splat(columns[step], step)
        scale = 1.0 / pivot
        pivots = jnp.where(row == step, pivot, pivots)
        others = jnp.where(row == step, 0.0, columns[step])
        for k in range(step + 1, panel_rows):
            columns[k] = columns[k] - others * (row_splat(columns[k], step) * scale)
        for k in range(step):
            forward[k] = jnp.where(row == step, full[k], forward[k])
            full[k] = full[k] - others * (row_splat(full[k], step) * scale)
        full[step] = full[step] - others * scale
    inverse_pivots = 1.0 / pivots
    root = lax.rsqrt(pivots)
    full = [column * inverse_pivots for column in full]
    forward = [column * root for column in forward]
    return full, forward


def combine(columns, rows):
    width = rows.shape[1] // lanes
    parts = []
    for part in range(width):
        piece = rows[:, part * lanes : (part + 1) * lanes]
        total = None
        for k, column in enumerate(columns):
            term = column * row_splat(piece, k)
            total = term if total is None else total + term
        parts.append(total)
    return jnp.concatenate(parts, axis=1)


def factor_kernel(scale, gram_ref, rows_ref, rotated_ref, upper_ref, factor_ref, inverse_ref):
    order = gram_ref.shape[0]
    factor_ref[...] = jnp.zeros((order, order), jnp.float32)
    inverse_ref[...] = jnp.zeros((order, order), jnp.float32)
    for start in range(0, order, block_rows):
        left = start // lanes * lanes
        right = left + lanes
        local = start - left
        row = lax.broadcasted_iota(jnp.int32, (block_rows, right), 0)
        col = lax.broadcasted_iota(jnp.int32, (block_rows, right), 1)
        unit = jnp.where(col == row + start, 1.0, 0.0).astype(jnp.float32)
        block = jnp.concatenate([gram_ref[start : start + block_rows, left:order], unit], axis=1)
        if start > 0:
            done = jnp.concatenate(
                [factor_ref[:start, left:order], inverse_ref[:start, :right]], axis=1
            )
            update = lax.dot_general(
                factor_ref[:start, left : left + lanes],
                done,
                (((0,), (0,)), ((), ())),
                precision=lax.Precision.HIGHEST,
                preferred_element_type=jnp.float32,
            )
            block = block - update[local : local + block_rows]
        groups = [
            block[g : g + panel_rows] for g in range(0, block_rows, panel_rows)
        ]
        for index in range(len(groups)):
            lane = local + index * panel_rows
            rows = groups[index]
            full, forward = panel_inverse([lane_splat(rows, lane + k) for k in range(panel_rows)])
            step_rows = combine(full, rows)
            for other in range(index + 1, len(groups)):
                target = groups[other]
                columns = [lane_splat(target, lane + k) for k in range(panel_rows)]
                groups[other] = target - combine(columns, step_rows)
            finished = combine(forward, rows)
            at = start + index * panel_rows
            factor_ref[at : at + panel_rows, left:order] = finished[:, : order - left]
            inverse_ref[at : at + panel_rows, :right] = finished[:, order - left :]
    row = lax.broadcasted_iota(jnp.int32, (order, order), 0)
    col = lax.broadcasted_iota(jnp.int32, (order, order), 1)
    upper_ref[...] = jnp.where(col >= row, factor_ref[...] * (1.0 / scale), 0.0)
    inverse = jnp.where(col <= row, inverse_ref[...] * scale, 0.0)
    high = inverse.astype(jnp.bfloat16)
    rest = inverse - high.astype(jnp.float32)
    middle = rest.astype(jnp.bfloat16)
    low = (rest - middle.astype(jnp.float32)).astype(jnp.bfloat16)
    count = rows_ref.shape[0]
    chunk = math.gcd(count, 512)
    for at in range(0, count, chunk):
        piece = rows_ref[at : at + chunk, :]
        total = jnp.zeros((chunk, order), jnp.float32)
        for part in (low, middle, high):
            total = total + lax.dot_general(
                piece, part, (((1,), (1,)), ((), ())), preferred_element_type=jnp.float32
            )
        rotated_ref[at : at + chunk, :] = total.astype(jnp.bfloat16)


def factor_and_rotate(gram_matrix, rows, total_cells):
    order = gram_matrix.shape[0]
    count = rows.shape[0]
    return pl.pallas_call(
        functools.partial(factor_kernel, math.sqrt(total_cells)),
        out_shape=(
            jax.ShapeDtypeStruct((count, order), jnp.bfloat16),
            jax.ShapeDtypeStruct((order, order), jnp.float32),
        ),
        scratch_shapes=[
            pltpu.VMEM((order, order), jnp.float32),
            pltpu.VMEM((order, order), jnp.float32),
        ],
        compiler_params=pltpu.CompilerParams(vmem_limit_bytes=vmem_limit),
    )(gram_matrix, rows)


def sum_over_devices(values):
    count = lax.axis_size(axes)
    order = values.shape[0]
    if order % count:
        return lax.psum(values, axes)
    share = order // count
    parts = lax.all_to_all(values.reshape(count, share, order), axes, 0, 0)
    total = jnp.sum(parts, axis=0)
    spread = jnp.broadcast_to(total[None], (count, share, order))
    return lax.all_to_all(spread, axes, 0, 0).reshape(order, order)


def shards(trial_orbitals, potential):
    layers, extent_y, extent_z, columns = trial_orbitals.shape
    bricks_x, bricks_y = lax.axis_size("gx"), lax.axis_size("gy")
    devices = bricks_x * bricks_y
    plane = extent_y * extent_z
    total_cells = devices * layers * plane
    weights = jnp.asarray(plane_weights(extent_y, extent_z))

    sent = split_columns(trial_orbitals.reshape(layers * plane, columns), devices, plane)
    received = lax.all_to_all(sent, axes, 0, 0)
    levels = jnp.broadcast_to(potential.reshape(1, layers, plane), (devices, layers, plane))
    levels = lax.all_to_all(levels, axes, 0, 0)
    filtered = filter_columns(received, levels, weights, bricks_x, bricks_y)
    received = lax.all_to_all(filtered, axes, 0, 0)
    rows, local_gram = join_columns(received, layers)
    gram_matrix = sum_over_devices(local_gram)
    rotated, upper_factor = factor_and_rotate(gram_matrix, rows, total_cells)
    return (rotated.reshape(trial_orbitals.shape), upper_factor)


def solution(mesh):
    placed = (P("gx", "gy", None, None), P("gx", "gy", None))
    return jax.shard_map(
        shards,
        mesh=mesh,
        in_specs=placed,
        out_specs=(P("gx", "gy", None, None), P()),
        check_vma=False,
    )
```

```python
import functools
import math

import jax
import jax.numpy as jnp
import ml_dtypes
import numpy as np
from jax import lax
from jax.experimental import pallas as pl
from jax.experimental.pallas import tpu as pltpu
from jax.sharding import Mesh, PartitionSpec as P

DEG = 3


STENCIL_WEIGHTS = (
    -5369.0 / 1800.0,
    12.0 / 7.0,
    -15.0 / 56.0,
    10.0 / 189.0,
    -1.0 / 112.0,
    2.0 / 1925.0,
    -1.0 / 16632.0,
)
stencil_reach = 6
filter_center = 11.5
filter_half = 8.5
axes = ("far", "near", "gy")
vmem_limit = 48 * 1024 * 1024

center_shift = -1.5 * STENCIL_WEIGHTS[0] - filter_center
side_weights = tuple(-0.5 * weight / filter_half for weight in STENCIL_WEIGHTS)


def exact_parts(values):
    parts = []
    rest = np.asarray(values, np.float32)
    for _ in range(3):
        part = rest.astype(ml_dtypes.bfloat16)
        parts.append(part)
        rest = rest - part.astype(np.float32)
    return np.stack(parts)


def plane_weights(extent_y, extent_z):
    def band(extent, shift):
        matrix = np.zeros((extent, extent), np.float64)
        for source in range(extent):
            for target in range(extent):
                distance = abs(target - (source + shift))
                if 1 <= distance <= stencil_reach:
                    matrix[source, target] = side_weights[distance]
        return matrix

    eye_y, eye_z = np.eye(extent_y), np.eye(extent_z)
    own = np.kron(band(extent_y, 0), eye_z) + np.kron(eye_y, band(extent_z, 0))
    before = np.kron(band(extent_y, -extent_y), eye_z)
    after = np.kron(band(extent_y, extent_y), eye_z)
    return np.stack([exact_parts(part) for part in (own, before, after)])


def split_kernel(cells_ref, sent_ref):
    devices, rows, plane = sent_ref.shape
    layers = cells_ref.shape[0] // plane
    share = rows // layers
    for layer in range(0, layers, 2):
        pair = []
        for at in (layer, layer + 1):
            block = cells_ref[at * plane : (at + 1) * plane, :].astype(jnp.float32)
            pair.append(block.T.reshape(devices, share, plane))
        both = jnp.concatenate(pair, axis=1)
        sent_ref[:, layer * share : (layer + 2) * share, :] = both.astype(jnp.bfloat16)


def split_columns(cells, devices, plane):
    count, columns = cells.shape
    layers = count // plane
    share = columns // devices
    if share % 8 == 0 and layers % 2 == 0:
        return pl.pallas_call(
            split_kernel,
            out_shape=jax.ShapeDtypeStruct((devices, layers * share, plane), jnp.bfloat16),
            compiler_params=pltpu.CompilerParams(vmem_limit_bytes=vmem_limit),
        )(cells)
    spread = cells.reshape(layers, plane, devices, share).transpose(2, 0, 3, 1)
    return spread.reshape(devices, layers * share, plane)


def join_kernel(received_ref, cells_ref, gram_ref):
    devices, rows, plane = received_ref.shape
    layers = cells_ref.shape[0] // plane
    share = rows // layers
    columns = devices * share
    total = None
    for layer in range(0, layers, 2):
        both = received_ref[:, layer * share : (layer + 2) * share, :].astype(jnp.float32)
        for side in range(2):
            block = both[:, side * share : (side + 1) * share, :].reshape(columns, plane)
            at = (layer + side) * plane
            cells_ref[at : at + plane, :] = block.T.astype(jnp.bfloat16)
            narrow = block.astype(jnp.bfloat16)
            part = lax.dot_general(
                narrow, narrow, (((1,), (1,)), ((), ())), preferred_element_type=jnp.float32
            )
            total = part if total is None else total + part
    half, quarter = columns // 2, columns // 4
    gram_ref[:half, :] = total[:half]
    gram_ref[half:, :half] = total[half : half + quarter, half:]
    gram_ref[half:, half:] = total[half + quarter :, half:]


def join_columns(received, layers):
    devices, rows, plane = received.shape
    share = rows // layers
    columns = devices * share
    if share % 8 == 0 and layers % 2 == 0:
        return pl.pallas_call(
            join_kernel,
            out_shape=(
                jax.ShapeDtypeStruct((layers * plane, columns), jnp.bfloat16),
                jax.ShapeDtypeStruct((columns // 4 * 3, columns), jnp.float32),
            ),
            compiler_params=pltpu.CompilerParams(vmem_limit_bytes=vmem_limit),
        )(received)
    cells = received.reshape(devices, layers, share, plane).transpose(1, 3, 0, 2)
    cells = cells.reshape(layers * plane, columns)
    gram = lax.dot_general(cells, cells, (((0,), (0,)), ((), ())), preferred_element_type=jnp.float32)
    half, quarter = columns // 2, columns // 4
    rest = jnp.concatenate([gram[half : half + quarter, half:], gram[half + quarter :, half:]], axis=1)
    return cells, jnp.concatenate([gram[:half], rest], axis=0)


def filter_kernel(
    bricks_x, bricks_y, received_ref, potential_ref, weights_ref, sent_ref,
    start_ref, first_ref, second_ref, plane_ref, center_ref,
):
    _, rows, plane = received_ref.shape
    layers = potential_ref.shape[1]
    share = rows // layers
    total = bricks_x * rows
    margin = stencil_reach * share
    for ref in (start_ref, first_ref, second_ref):
        ref[:margin, :] = jnp.zeros((margin, bricks_y * plane), jnp.float32)
        ref[margin + total :, :] = jnp.zeros((margin, bricks_y * plane), jnp.float32)
    for brick in range(bricks_x * bricks_y):
        at = margin + brick // bricks_y * rows
        lanes_at = brick % bricks_y * plane
        start_ref[at : at + rows, lanes_at : lanes_at + plane] = received_ref[brick].astype(jnp.float32)
        level = (potential_ref[brick] + center_shift) * (1.0 / filter_half)
        level = jnp.broadcast_to(level[:, None, :], (layers, share, plane)).reshape(rows, plane)
        center_ref[at - margin : at - margin + rows, lanes_at : lanes_at + plane] = level

    def apply(field_ref, write):
        narrow = [
            field_ref[margin : margin + total, b * plane : (b + 1) * plane].astype(jnp.bfloat16)
            for b in range(bricks_y)
        ]
        for b in range(bricks_y):
            fields, weights = [], []
            for kind, other in ((0, b), (1, b - 1), (2, b + 1)):
                if 0 <= other < bricks_y:
                    for part in range(weights_ref.shape[1]):
                        fields.append(narrow[other])
                        weights.append(weights_ref[kind, part])
            plane_ref[:, b * plane : (b + 1) * plane] = jnp.dot(
                jnp.concatenate(fields, axis=1),
                jnp.concatenate(weights, axis=0),
                preferred_element_type=jnp.float32,
            )

        def one_brick(brick, at):
            for b in range(bricks_y):
                here = slice(b * plane, (b + 1) * plane)
                window = field_ref[pl.ds(at, rows + 2 * margin), here]
                value = center_ref[pl.ds(at, rows), here] * window[margin : margin + rows]
                value = value + plane_ref[pl.ds(at, rows), here]
                for distance in range(1, stencil_reach + 1):
                    low = margin - distance * share
                    high = margin + distance * share
                    pair = window[low : low + rows] + window[high : high + rows]
                    value = value + side_weights[distance] * pair
                write(brick, b, at, here, value)

        if rows % 8 == 0:
            @pl.loop(0, bricks_x)
            def _(brick):
                one_brick(brick, pl.multiple_of(brick * rows, 8))
        else:
            for brick in range(bricks_x):
                one_brick(brick, brick * rows)

    def write_first(brick, b, at, here, value):
        first_ref[pl.ds(at + margin, rows), here] = value.astype(jnp.bfloat16).astype(jnp.float32)

    def write_second(brick, b, at, here, value):
        following = 2.0 * value - start_ref[pl.ds(at + margin, rows), here]
        second_ref[pl.ds(at + margin, rows), here] = following.astype(jnp.bfloat16).astype(jnp.float32)

    def write_third(brick, b, at, here, value):
        following = 2.0 * value - first_ref[pl.ds(at + margin, rows), here]
        sent_ref[brick * bricks_y + b] = following.astype(jnp.bfloat16)

    apply(start_ref, write_first)
    apply(first_ref, write_second)
    apply(second_ref, write_third)


def filter_columns(received, potential, weights, bricks_x, bricks_y):
    _, rows, plane = received.shape
    share = rows // potential.shape[1]
    total = bricks_x * rows
    padded = total + 2 * stencil_reach * share
    width = bricks_y * plane
    field = pltpu.VMEM((padded, width), jnp.float32)
    whole = pltpu.VMEM((total, width), jnp.float32)
    return pl.pallas_call(
        functools.partial(filter_kernel, bricks_x, bricks_y),
        out_shape=jax.ShapeDtypeStruct(received.shape, jnp.bfloat16),
        scratch_shapes=[field, field, field, whole, whole],
        compiler_params=pltpu.CompilerParams(vmem_limit_bytes=vmem_limit),
    )(received, potential, weights)


lanes = 128
panel_rows = 8
block_rows = 64


def row_splat(values, row):
    return jnp.broadcast_to(values[row : row + 1, :], values.shape)


def lane_splat(values, lane):
    return jnp.broadcast_to(values[:, lane : lane + 1], (panel_rows, lanes))


def panel_inverse(columns):
    row = lax.broadcasted_iota(jnp.int32, (panel_rows, lanes), 0)
    columns = list(columns)
    full = [jnp.where(row == k, 1.0, 0.0).astype(jnp.float32) for k in range(panel_rows)]
    forward = list(full)
    pivots = jnp.zeros((panel_rows, lanes), jnp.float32)
    for step in range(panel_rows):
        pivot = row_splat(columns[step], step)
        scale = 1.0 / pivot
        pivots = jnp.where(row == step, pivot, pivots)
        others = jnp.where(row == step, 0.0, columns[step])
        for k in range(step + 1, panel_rows):
            columns[k] = columns[k] - others * (row_splat(columns[k], step) * scale)
        for k in range(step):
            forward[k] = jnp.where(row == step, full[k], forward[k])
            full[k] = full[k] - others * (row_splat(full[k], step) * scale)
        full[step] = full[step] - others * scale
    inverse_pivots = 1.0 / pivots
    root = lax.rsqrt(pivots)
    full = [column * inverse_pivots for column in full]
    forward = [column * root for column in forward]
    return full, forward


def combine(columns, rows):
    width = rows.shape[1] // lanes
    parts = []
    for part in range(width):
        piece = rows[:, part * lanes : (part + 1) * lanes]
        total = None
        for k, column in enumerate(columns):
            term = column * row_splat(piece, k)
            total = term if total is None else total + term
        parts.append(total)
    return jnp.concatenate(parts, axis=1)


def factor_kernel(scale, gram_ref, rows_ref, rotated_ref, upper_ref, factor_ref, inverse_ref):
    order = gram_ref.shape[1]
    half, quarter = order // 2, order // 4
    factor_ref[...] = jnp.zeros((order, order), jnp.float32)
    inverse_ref[...] = jnp.zeros((order, order), jnp.float32)
    for start in range(0, order, block_rows):
        left = start // lanes * lanes
        right = left + lanes
        local = start - left
        row = lax.broadcasted_iota(jnp.int32, (block_rows, right), 0)
        col = lax.broadcasted_iota(jnp.int32, (block_rows, right), 1)
        unit = jnp.where(col == row + start, 1.0, 0.0).astype(jnp.float32)
        if start < half:
            own = gram_ref[start : start + block_rows, :]
        else:
            side = (start - half) // quarter * half
            at = half + (start - half) % quarter
            own = gram_ref[at : at + block_rows, side : side + half]
        block = jnp.concatenate([own, unit], axis=1)
        if start > 0:
            done = jnp.concatenate(
                [factor_ref[:start, left:order], inverse_ref[:start, :right]], axis=1
            )
            update = lax.dot_general(
                factor_ref[:start, left : left + lanes],
                done,
                (((0,), (0,)), ((), ())),
                precision=lax.Precision.HIGHEST,
                preferred_element_type=jnp.float32,
            )
            block = block - update[local : local + block_rows]
        groups = [
            block[g : g + panel_rows] for g in range(0, block_rows, panel_rows)
        ]
        for index in range(len(groups)):
            lane = local + index * panel_rows
            rows = groups[index]
            full, forward = panel_inverse([lane_splat(rows, lane + k) for k in range(panel_rows)])
            step_rows = combine(full, rows)
            for other in range(index + 1, len(groups)):
                target = groups[other]
                columns = [lane_splat(target, lane + k) for k in range(panel_rows)]
                groups[other] = target - combine(columns, step_rows)
            finished = combine(forward, rows)
            at = start + index * panel_rows
            factor_ref[at : at + panel_rows, left:order] = finished[:, : order - left]
            inverse_ref[at : at + panel_rows, :right] = finished[:, order - left :]
    row = lax.broadcasted_iota(jnp.int32, (order, order), 0)
    col = lax.broadcasted_iota(jnp.int32, (order, order), 1)
    upper_ref[...] = jnp.where(col >= row, factor_ref[...] * (1.0 / scale), 0.0)
    inverse = jnp.where(col <= row, inverse_ref[...] * scale, 0.0)
    high = inverse.astype(jnp.bfloat16)
    rest = inverse - high.astype(jnp.float32)
    middle = rest.astype(jnp.bfloat16)
    low = (rest - middle.astype(jnp.float32)).astype(jnp.bfloat16)
    count = rows_ref.shape[0]
    chunk = math.gcd(count, 512)
    for at in range(0, count, chunk):
        piece = rows_ref[at : at + chunk, :]
        total = jnp.zeros((chunk, order), jnp.float32)
        for part in (low, middle, high):
            total = total + lax.dot_general(
                piece, part, (((1,), (1,)), ((), ())), preferred_element_type=jnp.float32
            )
        rotated_ref[at : at + chunk, :] = total.astype(jnp.bfloat16)


def factor_and_rotate(gram_matrix, rows, total_cells):
    order = gram_matrix.shape[1]
    count = rows.shape[0]
    return pl.pallas_call(
        functools.partial(factor_kernel, math.sqrt(total_cells)),
        out_shape=(
            jax.ShapeDtypeStruct((count, order), jnp.bfloat16),
            jax.ShapeDtypeStruct((order, order), jnp.float32),
        ),
        scratch_shapes=[
            pltpu.VMEM((order, order), jnp.float32),
            pltpu.VMEM((order, order), jnp.float32),
        ],
        compiler_params=pltpu.CompilerParams(vmem_limit_bytes=vmem_limit),
    )(gram_matrix, rows)


def sum_over_devices(values):
    plane_axes = ("near", "gy")
    plane, planes = lax.axis_size(plane_axes), lax.axis_size("far")
    count, order = values.shape
    if count % plane:
        return lax.psum(values, axes)
    share = count // plane
    parts = lax.all_to_all(values.reshape(plane, share, order), plane_axes, 0, 0)
    total = jnp.sum(parts, axis=0)
    spread = jnp.broadcast_to(total[None], (planes, share, order))
    total = jnp.sum(lax.all_to_all(spread, "far", 0, 0), axis=0)
    spread = jnp.broadcast_to(total[None], (plane, share, order))
    return lax.all_to_all(spread, plane_axes, 0, 0).reshape(count, order)


def shards(trial_orbitals, potential):
    layers, extent_y, extent_z, columns = trial_orbitals.shape
    bricks_x, bricks_y = lax.axis_size(("far", "near")), lax.axis_size("gy")
    devices = bricks_x * bricks_y
    plane = extent_y * extent_z
    total_cells = devices * layers * plane
    weights = jnp.asarray(plane_weights(extent_y, extent_z))

    sent = split_columns(trial_orbitals.reshape(layers * plane, columns), devices, plane)
    received = lax.all_to_all(sent, axes, 0, 0)
    levels = lax.all_gather(potential.reshape(layers, plane), axes)
    filtered = filter_columns(received, levels, weights, bricks_x, bricks_y)
    received = lax.all_to_all(filtered, axes, 0, 0)
    rows, local_gram = join_columns(received, layers)
    gram_matrix = sum_over_devices(local_gram)
    rotated, upper_factor = factor_and_rotate(gram_matrix, rows, total_cells)
    return (rotated.reshape(trial_orbitals.shape), upper_factor)


def solution(mesh):
    bricks_x, bricks_y = mesh.devices.shape
    near = math.gcd(bricks_x, 4)
    cut = Mesh(mesh.devices.reshape(bricks_x // near, near, bricks_y), axes)
    cells = P(("far", "near"), "gy")
    return jax.shard_map(
        shards,
        mesh=cut,
        in_specs=(cells, cells),
        out_specs=(cells, P()),
        check_vma=False,
    )
```

```python
import functools
import math

import jax
import jax.numpy as jnp
import ml_dtypes
import numpy as np
from jax import lax
from jax.experimental import pallas as pl
from jax.experimental.pallas import tpu as pltpu
from jax.sharding import Mesh, PartitionSpec as P

DEG = 3


STENCIL_WEIGHTS = (
    -5369.0 / 1800.0,
    12.0 / 7.0,
    -15.0 / 56.0,
    10.0 / 189.0,
    -1.0 / 112.0,
    2.0 / 1925.0,
    -1.0 / 16632.0,
)
stencil_reach = 6
filter_center = 11.5
filter_half = 8.5
axes = ("far", "mid", "core", "gy")
owned = 2
group = 16
vmem_limit = 48 * 1024 * 1024

center_shift = -1.5 * STENCIL_WEIGHTS[0] - filter_center
side_weights = tuple(-0.5 * weight / filter_half for weight in STENCIL_WEIGHTS)


def bfloat16_parts(values):
    parts = []
    rest = np.asarray(values, np.float32)
    for _ in range(3):
        part = rest.astype(ml_dtypes.bfloat16)
        parts.append(part)
        rest = rest - part.astype(np.float32)
    return np.stack(parts)


def plane_weights(extent_y, extent_z):
    def band(extent, shift):
        matrix = np.zeros((extent, extent), np.float64)
        for source in range(extent):
            for target in range(extent):
                distance = abs(target - (source + shift))
                if 1 <= distance <= stencil_reach:
                    matrix[source, target] = side_weights[distance]
        return matrix

    eye_y, eye_z = np.eye(extent_y), np.eye(extent_z)
    own = np.kron(band(extent_y, 0), eye_z) + np.kron(eye_y, band(extent_z, 0))
    before = np.kron(band(extent_y, -extent_y), eye_z)
    after = np.kron(band(extent_y, extent_y), eye_z)
    return np.stack([bfloat16_parts(part) for part in (own, before, after)])


def level_rows(potential, rows):
    rest = (potential + center_shift) * (1.0 / filter_half)
    parts = []
    for _ in range(3):
        part = rest.astype(jnp.bfloat16).astype(jnp.float32)
        parts.append(part)
        rest = rest - part
    unused = jnp.zeros((rows - 3 * rest.shape[0], rest.shape[1]), jnp.float32)
    return jnp.concatenate(parts + [unused], axis=0).astype(jnp.bfloat16)


def level_room(layers):
    return -(-3 * layers // 16) * 16


def offsets(bricks_y):
    return [(i, j) for i in range(owned) for j in range(bricks_y)]


def ahead(mid, y, step, bricks_y):
    return lax.rem(mid + step[0], owned), lax.rem(y + step[1], bricks_y)


def behind(mid, y, step, bricks_y):
    return lax.rem(mid + step[0], owned), lax.rem(y - step[1] + bricks_y, bricks_y)


def exchange(messages, bricks_y):
    result = [messages[0]]
    for step, message in list(zip(offsets(bricks_y), messages))[1:]:
        perm = []
        for mid in range(owned):
            for y in range(bricks_y):
                target = (mid + step[0]) % owned * bricks_y + (y + step[1]) % bricks_y
                perm.append((mid * bricks_y + y, target))
        result.append(lax.ppermute(message, ("mid", "gy"), perm))
    return result


def split_kernel(bricks_y, cells_ref, potential_ref, *refs):
    sent_refs, block_ref = refs[:-1], refs[-1]
    mid, y = lax.axis_index("mid"), lax.axis_index("gy")
    columns, plane = block_ref.shape
    share = columns // len(sent_refs)
    layers = cells_ref.shape[0] // plane
    potential = jnp.concatenate(
        [potential_ref[:, at, :] for at in range(potential_ref.shape[1])], axis=1
    )
    extra = level_rows(potential, sent_refs[0].shape[0] - layers * share)
    for sent_ref in sent_refs:
        sent_ref[layers * share :, :] = extra
    for layer in range(layers):
        block = cells_ref[layer * plane : (layer + 1) * plane, :].astype(jnp.float32)
        block_ref[...] = block.T
        for step, sent_ref in zip(offsets(bricks_y), sent_refs):
            to_mid, to_y = ahead(mid, y, step, bricks_y)
            first = pl.multiple_of((to_mid * bricks_y + to_y) * share, share)
            own = block_ref[pl.ds(first, share), :]
            sent_ref[layer * share : (layer + 1) * share, :] = own.astype(jnp.bfloat16)


def split_columns(cells, potential, bricks_y):
    count, columns = cells.shape
    layers = potential.shape[0]
    plane = count // layers
    parts = owned * bricks_y
    message = jax.ShapeDtypeStruct(
        (layers * (columns // parts) + level_room(layers), plane), jnp.bfloat16
    )
    return pl.pallas_call(
        functools.partial(split_kernel, bricks_y),
        out_shape=[message] * parts,
        scratch_shapes=[pltpu.VMEM((columns, plane), jnp.float32)],
        compiler_params=pltpu.CompilerParams(vmem_limit_bytes=vmem_limit),
    )(cells, potential)


def place_kernel(bricks_y, *refs):
    parts = owned * bricks_y
    received_refs, (own_ref, level_ref, edge_ref) = refs[:parts], refs[parts:]
    mid, y = lax.axis_index("mid"), lax.axis_index("gy")
    rows = own_ref.shape[2]
    layers = level_ref.shape[2]
    for step, received_ref in zip(offsets(bricks_y), received_refs):
        at, b = behind(mid, y, step, bricks_y)
        own_ref[at, b] = received_ref[:rows]
        extra = received_ref[rows:].astype(jnp.float32)
        level = extra[:layers] + extra[layers : 2 * layers] + extra[2 * layers : 3 * layers]
        level_ref[at, b] = level
    edge_ref[...] = own_ref[lax.axis_index("core")]


def place(received, layers, bricks_y):
    plane = received[0].shape[1]
    rows = received[0].shape[0] - level_room(layers)
    return pl.pallas_call(
        functools.partial(place_kernel, bricks_y),
        out_shape=(
            jax.ShapeDtypeStruct((owned, bricks_y, rows, plane), jnp.bfloat16),
            jax.ShapeDtypeStruct((owned, bricks_y, layers, plane), jnp.float32),
            jax.ShapeDtypeStruct((bricks_y, rows, plane), jnp.bfloat16),
        ),
        compiler_params=pltpu.CompilerParams(vmem_limit_bytes=vmem_limit),
    )(*received)


def plane_kernel(own_ref, level_ref, weights_ref, partial_ref):
    _, bricks_y, rows, plane = own_ref.shape
    layers = level_ref.shape[2]
    share = rows // layers
    for b in range(bricks_y):
        fields, weights = [], []
        for kind, other in ((0, b), (1, b - 1), (2, b + 1)):
            if 0 <= other < bricks_y:
                for part in range(weights_ref.shape[1]):
                    fields.append(own_ref[:, other].reshape(owned * rows, plane))
                    weights.append(weights_ref[kind, part])
        sides = jnp.dot(
            jnp.concatenate(fields, axis=1),
            jnp.concatenate(weights, axis=0),
            preferred_element_type=jnp.float32,
        )
        for a in range(owned):
            for layer in range(layers):
                here = slice(layer * share, (layer + 1) * share)
                center = own_ref[a, b, here].astype(jnp.float32)
                level = jnp.broadcast_to(level_ref[a, b, layer : layer + 1, :], (share, plane))
                side = sides[a * rows + layer * share : a * rows + (layer + 1) * share]
                partial_ref[a, b, here] = side + level * center


def plane_part(own, level, weights):
    _, bricks_y, rows, plane = own.shape
    flops = 2 * owned * bricks_y * bricks_y * 3 * rows * plane * plane
    return pl.pallas_call(
        plane_kernel,
        out_shape=jax.ShapeDtypeStruct(own.shape, jnp.float32),
        cost_estimate=pl.CostEstimate(flops=flops, bytes_accessed=own.size * 6, transcendentals=0),
        compiler_params=pltpu.CompilerParams(vmem_limit_bytes=vmem_limit),
    )(own, level, weights)


def layer_kernel(stage, layers, partial_ref, own_ref, swapped_ref, edge_ref, *refs):
    if stage == 0:
        before_ref, (next_ref, next_edge_ref) = None, refs
    else:
        before_ref, refs = refs[0], refs[1:]
        if stage == DEG - 1:
            sent_refs, next_ref = refs[:-1], refs[-1]
        else:
            next_ref, next_edge_ref = refs
    core, mid, y = lax.axis_index("core"), lax.axis_index("mid"), lax.axis_index("gy")
    _, bricks_y, rows, plane = own_ref.shape
    share = rows // layers
    width = min(plane, 128)

    def chosen(first, second):
        return jnp.where(core == 0, first.astype(jnp.float32), second.astype(jnp.float32))

    for a in range(owned):
        for b in range(bricks_y):
            for column in range(0, share, group):
                for left in range(0, plane, width):
                    lane = slice(left, left + width)

                    def rows_of(layer):
                        return slice(layer * share + column, layer * share + column + group)

                    low, own, high = [], [], []
                    for layer in range(layers):
                        here = rows_of(layer)
                        own.append(own_ref[a, b, here, lane].astype(jnp.float32))
                        near = swapped_ref[core, b, here, lane].astype(jnp.float32)
                        if a == 0:
                            low.append(chosen(edge_ref[b, here, lane], swapped_ref[0, b, here, lane]))
                            high.append(near)
                        else:
                            low.append(near)
                            high.append(chosen(swapped_ref[1, b, here, lane], edge_ref[b, here, lane]))
                    window = low + own + high
                    for layer in range(layers):
                        here = rows_of(layer)
                        value = partial_ref[a, b, here, lane]
                        for distance in range(1, stencil_reach + 1):
                            pair = window[layers + layer - distance] + window[layers + layer + distance]
                            value = value + side_weights[distance] * pair
                        if stage > 0:
                            value = 2.0 * value - before_ref[a, b, here, lane].astype(jnp.float32)
                        next_ref[a, b, here, lane] = value.astype(jnp.bfloat16)
    if stage < DEG - 1:
        next_edge_ref[...] = next_ref[core]
    else:
        for step, sent_ref in zip(offsets(bricks_y), sent_refs):
            to_mid, to_y = ahead(mid, y, step, bricks_y)
            sent_ref[...] = next_ref[to_mid, to_y]


def layer_part(stage, layers, partial, own, swapped, edge, before):
    _, bricks_y, rows, plane = own.shape
    whole = jax.ShapeDtypeStruct(own.shape, jnp.bfloat16)
    one = jax.ShapeDtypeStruct((rows, plane), jnp.bfloat16)
    last = stage == DEG - 1
    return pl.pallas_call(
        functools.partial(layer_kernel, stage, layers),
        out_shape=[one] * (owned * bricks_y) if last else [whole, jax.ShapeDtypeStruct(edge.shape, jnp.bfloat16)],
        scratch_shapes=[pltpu.VMEM(own.shape, jnp.bfloat16)] if last else [],
        compiler_params=pltpu.CompilerParams(vmem_limit_bytes=vmem_limit),
    )(partial, own, swapped, edge, *([] if stage == 0 else [before]))


def neighbour_bricks(own, edge):
    count = lax.axis_size(("far", "core"))
    pairs = [(at, at + 1) for at in range(1, count - 1, 2)]
    edge = lax.ppermute(edge, ("far", "core"), pairs + [(b, a) for a, b in pairs])
    return lax.ppermute(own, "core", [(0, 1), (1, 0)]), edge


def chebyshev(own, level, edge, weights):
    layers = level.shape[2]
    before = None
    for stage in range(DEG):
        swapped, arrived = neighbour_bricks(own, edge)
        partial = plane_part(own, level, weights)
        result = layer_part(stage, layers, partial, own, swapped, arrived, before)
        if stage < DEG - 1:
            before, (own, edge) = own, result
    return result


def join_kernel(bricks_y, *refs):
    parts = owned * bricks_y
    received_refs, (cells_ref, gram_ref, block_ref) = refs[:parts], refs[parts:]
    mid, y = lax.axis_index("mid"), lax.axis_index("gy")
    columns, plane = block_ref.shape
    share = columns // parts
    layers = cells_ref.shape[0] // plane
    total = None
    for layer in range(layers):
        for step, received_ref in zip(offsets(bricks_y), received_refs):
            from_mid, from_y = behind(mid, y, step, bricks_y)
            first = pl.multiple_of((from_mid * bricks_y + from_y) * share, share)
            own = received_ref[layer * share : (layer + 1) * share, :]
            block_ref[pl.ds(first, share), :] = own.astype(jnp.float32)
        block = block_ref[...]
        cells_ref[layer * plane : (layer + 1) * plane, :] = block.T.astype(jnp.bfloat16)
        narrow = block.astype(jnp.bfloat16)
        part = lax.dot_general(
            narrow, narrow, (((1,), (1,)), ((), ())), preferred_element_type=jnp.float32
        )
        total = part if total is None else total + part
    half = columns // 2
    packed = jnp.concatenate([total[:half], total[half:, half:]], axis=1)
    piece = gram_ref.shape[1]
    for device in range(gram_ref.shape[0]):
        gram_ref[device] = packed[device * piece : (device + 1) * piece]


def join_columns(received, layers, bricks_y):
    rows, plane = received[0].shape
    columns = rows // layers * owned * bricks_y
    half = columns // 2
    shares = math.gcd(lax.axis_size(axes), half)
    return pl.pallas_call(
        functools.partial(join_kernel, bricks_y),
        out_shape=(
            jax.ShapeDtypeStruct((layers * plane, columns), jnp.bfloat16),
            jax.ShapeDtypeStruct((shares, half // shares, 3 * half), jnp.float32),
        ),
        scratch_shapes=[pltpu.VMEM((columns, plane), jnp.float32)],
        compiler_params=pltpu.CompilerParams(vmem_limit_bytes=vmem_limit),
    )(*received)


lanes = 128
panel_rows = 8
block_rows = 64


def row_splat(values, row):
    return jnp.broadcast_to(values[row : row + 1, :], values.shape)


def lane_splat(values, lane):
    return jnp.broadcast_to(values[:, lane : lane + 1], (panel_rows, lanes))


def panel_inverse(columns):
    row = lax.broadcasted_iota(jnp.int32, (panel_rows, lanes), 0)
    columns = list(columns)
    full = [jnp.where(row == k, 1.0, 0.0).astype(jnp.float32) for k in range(panel_rows)]
    forward = list(full)
    pivots = jnp.zeros((panel_rows, lanes), jnp.float32)
    for step in range(panel_rows):
        pivot = row_splat(columns[step], step)
        scale = 1.0 / pivot
        pivots = jnp.where(row == step, pivot, pivots)
        others = jnp.where(row == step, 0.0, columns[step])
        for k in range(step + 1, panel_rows):
            columns[k] = columns[k] - others * (row_splat(columns[k], step) * scale)
        for k in range(step):
            forward[k] = jnp.where(row == step, full[k], forward[k])
            full[k] = full[k] - others * (row_splat(full[k], step) * scale)
        full[step] = full[step] - others * scale
    inverse_pivots = 1.0 / pivots
    root = lax.rsqrt(pivots)
    full = [column * inverse_pivots for column in full]
    forward = [column * root for column in forward]
    return full, forward


def combine(columns, rows):
    width = rows.shape[1] // lanes
    parts = []
    for part in range(width):
        piece = rows[:, part * lanes : (part + 1) * lanes]
        total = None
        for k, column in enumerate(columns):
            term = column * row_splat(piece, k)
            total = term if total is None else total + term
        parts.append(total)
    return jnp.concatenate(parts, axis=1)


def factor_kernel(scale, gram_ref, rows_ref, rotated_ref, upper_ref, packed_ref, factor_ref, inverse_ref):
    shares, piece, width = gram_ref.shape
    half = shares * piece
    order = 2 * half
    for share in range(shares):
        packed_ref[share * piece : (share + 1) * piece, :] = gram_ref[share]
    factor_ref[...] = jnp.zeros((order, order), jnp.float32)
    inverse_ref[...] = jnp.zeros((order, order), jnp.float32)
    for start in range(0, order, block_rows):
        left = start // lanes * lanes
        right = left + lanes
        local = start - left
        row = lax.broadcasted_iota(jnp.int32, (block_rows, right), 0)
        col = lax.broadcasted_iota(jnp.int32, (block_rows, right), 1)
        unit = jnp.where(col == row + start, 1.0, 0.0).astype(jnp.float32)
        at, side = (start, 0) if start < half else (start - half, order)
        own = packed_ref[at : at + block_rows, side : side + order - left]
        block = jnp.concatenate([own, unit], axis=1)
        if start > 0:
            done = jnp.concatenate(
                [factor_ref[:start, left:order], inverse_ref[:start, :right]], axis=1
            )
            update = lax.dot_general(
                factor_ref[:start, left : left + lanes],
                done,
                (((0,), (0,)), ((), ())),
                precision=lax.Precision.HIGHEST,
                preferred_element_type=jnp.float32,
            )
            block = block - update[local : local + block_rows]
        groups = [
            block[g : g + panel_rows] for g in range(0, block_rows, panel_rows)
        ]
        for index in range(len(groups)):
            lane = local + index * panel_rows
            rows = groups[index]
            full, forward = panel_inverse([lane_splat(rows, lane + k) for k in range(panel_rows)])
            step_rows = combine(full, rows)
            for other in range(index + 1, len(groups)):
                target = groups[other]
                columns = [lane_splat(target, lane + k) for k in range(panel_rows)]
                groups[other] = target - combine(columns, step_rows)
            finished = combine(forward, rows)
            at = start + index * panel_rows
            factor_ref[at : at + panel_rows, left:order] = finished[:, : order - left]
            inverse_ref[at : at + panel_rows, :right] = finished[:, order - left :]
    row = lax.broadcasted_iota(jnp.int32, (order, order), 0)
    col = lax.broadcasted_iota(jnp.int32, (order, order), 1)
    upper_ref[...] = jnp.where(col >= row, factor_ref[...] * (1.0 / scale), 0.0)
    inverse = jnp.where(col <= row, inverse_ref[...] * scale, 0.0)
    high = inverse.astype(jnp.bfloat16)
    rest = inverse - high.astype(jnp.float32)
    middle = rest.astype(jnp.bfloat16)
    low = (rest - middle.astype(jnp.float32)).astype(jnp.bfloat16)
    count = rows_ref.shape[0]
    chunk = math.gcd(count, 512)
    for at in range(0, count, chunk):
        piece = rows_ref[at : at + chunk, :]
        total = jnp.zeros((chunk, order), jnp.float32)
        for part in (low, middle, high):
            total = total + lax.dot_general(
                piece, part, (((1,), (1,)), ((), ())), preferred_element_type=jnp.float32
            )
        rotated_ref[at : at + chunk, :] = total.astype(jnp.bfloat16)


def factor_and_rotate(gram_matrix, rows, total_cells):
    order = rows.shape[1]
    count = rows.shape[0]
    return pl.pallas_call(
        functools.partial(factor_kernel, math.sqrt(total_cells)),
        out_shape=(
            jax.ShapeDtypeStruct((count, order), jnp.bfloat16),
            jax.ShapeDtypeStruct((order, order), jnp.float32),
        ),
        scratch_shapes=[
            pltpu.VMEM((order // 2, order // 2 * 3), jnp.float32),
            pltpu.VMEM((order, order), jnp.float32),
            pltpu.VMEM((order, order), jnp.float32),
        ],
        compiler_params=pltpu.CompilerParams(vmem_limit_bytes=vmem_limit),
    )(gram_matrix, rows)


def sum_over_devices(values):
    if lax.axis_size(axes) != values.shape[0]:
        return lax.psum(values, axes)
    total = jnp.sum(lax.all_to_all(values, axes, 0, 0), axis=0)
    return lax.all_to_all(jnp.broadcast_to(total[None], values.shape), axes, 0, 0)


def shards(trial_orbitals, potential):
    layers, extent_y, extent_z, columns = trial_orbitals.shape
    bricks_y = lax.axis_size("gy")
    total_cells = lax.axis_size(axes) * layers * extent_y * extent_z
    weights = jnp.asarray(plane_weights(extent_y, extent_z))

    cells = trial_orbitals.reshape(layers * extent_y * extent_z, columns)
    sent = split_columns(cells, potential, bricks_y)
    own, level, edge = place(exchange(sent, bricks_y), layers, bricks_y)
    sent = chebyshev(own, level, edge, weights)
    rows, local_gram = join_columns(exchange(sent, bricks_y), layers, bricks_y)
    gram_matrix = sum_over_devices(local_gram)
    rotated, upper_factor = factor_and_rotate(gram_matrix, rows, total_cells)
    return (rotated.reshape(trial_orbitals.shape), upper_factor)


def solution(mesh):
    bricks_x, bricks_y = mesh.devices.shape
    cut = Mesh(mesh.devices.reshape(bricks_x // 4, owned, 2, bricks_y), axes)
    cells = P(("far", "mid", "core"), "gy")
    return jax.shard_map(
        shards,
        mesh=cut,
        in_specs=(cells, cells),
        out_specs=(cells, P()),
        check_vma=False,
    )
```

```python
import functools
import math

import jax
import jax.numpy as jnp
import ml_dtypes
import numpy as np
from jax import lax
from jax.experimental import pallas as pl
from jax.experimental.pallas import tpu as pltpu
from jax.sharding import Mesh, PartitionSpec as P

DEG = 3


STENCIL_WEIGHTS = (
    -5369.0 / 1800.0,
    12.0 / 7.0,
    -15.0 / 56.0,
    10.0 / 189.0,
    -1.0 / 112.0,
    2.0 / 1925.0,
    -1.0 / 16632.0,
)
stencil_reach = 6
filter_center = 11.5
filter_half = 8.5
axes = ("far", "mid", "core", "gy")
owned = 2
group = 16
vmem_limit = 48 * 1024 * 1024
fetching_limit = 63 * 1024 * 1024

center_shift = -1.5 * STENCIL_WEIGHTS[0] - filter_center
side_weights = tuple(-0.5 * weight / filter_half for weight in STENCIL_WEIGHTS)


def bfloat16_parts(values):
    parts = []
    rest = np.asarray(values, np.float32)
    for _ in range(3):
        part = rest.astype(ml_dtypes.bfloat16)
        parts.append(part)
        rest = rest - part.astype(np.float32)
    return np.stack(parts)


def plane_weights(extent_y, extent_z):
    def band(extent, shift):
        matrix = np.zeros((extent, extent), np.float64)
        for source in range(extent):
            for target in range(extent):
                distance = abs(target - (source + shift))
                if 1 <= distance <= stencil_reach:
                    matrix[source, target] = side_weights[distance]
        return matrix

    eye_y, eye_z = np.eye(extent_y), np.eye(extent_z)
    own = np.kron(band(extent_y, 0), eye_z) + np.kron(eye_y, band(extent_z, 0))
    before = np.kron(band(extent_y, -extent_y), eye_z)
    after = np.kron(band(extent_y, extent_y), eye_z)
    return np.stack([bfloat16_parts(part) for part in (own, before, after)])


def level_rows(potential, rows):
    rest = (potential + center_shift) * (1.0 / filter_half)
    parts = []
    for _ in range(3):
        part = rest.astype(jnp.bfloat16).astype(jnp.float32)
        parts.append(part)
        rest = rest - part
    unused = jnp.zeros((rows - 3 * rest.shape[0], rest.shape[1]), jnp.float32)
    return jnp.concatenate(parts + [unused], axis=0).astype(jnp.bfloat16)


def level_room(layers):
    return -(-3 * layers // 16) * 16


def offsets(bricks_y):
    return [(i, j) for i in range(owned) for j in range(bricks_y)]


def ahead(mid, y, step, bricks_y):
    return lax.rem(mid + step[0], owned), lax.rem(y + step[1], bricks_y)


def behind(mid, y, step, bricks_y):
    return lax.rem(mid + step[0], owned), lax.rem(y - step[1] + bricks_y, bricks_y)


def exchange(messages, bricks_y):
    result = [messages[0]]
    for step, message in list(zip(offsets(bricks_y), messages))[1:]:
        perm = []
        for mid in range(owned):
            for y in range(bricks_y):
                target = (mid + step[0]) % owned * bricks_y + (y + step[1]) % bricks_y
                perm.append((mid * bricks_y + y, target))
        result.append(lax.ppermute(message, ("mid", "gy"), perm))
    return result


def split_kernel(bricks_y, cells_ref, potential_ref, *refs):
    sent_refs, (block_ref, fetched_ref, level_ref, arrived) = refs[:-4], refs[-4:]
    mid, y = lax.axis_index("mid"), lax.axis_index("gy")
    columns, plane = block_ref.shape
    share = columns // len(sent_refs)
    layers = cells_ref.shape[0] // plane
    fetches = [pltpu.make_async_copy(potential_ref, level_ref, arrived.at[layers])]
    for layer in range(layers):
        part = pl.ds(layer * plane, plane)
        fetches.append(
            pltpu.make_async_copy(cells_ref.at[part], fetched_ref.at[part], arrived.at[layer])
        )
    for fetch in fetches:
        fetch.start()
    fetches[0].wait()
    potential = jnp.concatenate(
        [level_ref[:, at, :] for at in range(level_ref.shape[1])], axis=1
    )
    extra = level_rows(potential, sent_refs[0].shape[0] - layers * share)
    for sent_ref in sent_refs:
        sent_ref[layers * share :, :] = extra
    for layer in range(layers):
        fetches[layer + 1].wait()
        block = fetched_ref[layer * plane : (layer + 1) * plane, :].astype(jnp.float32)
        block_ref[...] = block.T
        for step, sent_ref in zip(offsets(bricks_y), sent_refs):
            to_mid, to_y = ahead(mid, y, step, bricks_y)
            first = pl.multiple_of((to_mid * bricks_y + to_y) * share, share)
            own = block_ref[pl.ds(first, share), :]
            sent_ref[layer * share : (layer + 1) * share, :] = own.astype(jnp.bfloat16)


def split_columns(cells, potential, bricks_y):
    count, columns = cells.shape
    layers = potential.shape[0]
    plane = count // layers
    parts = owned * bricks_y
    message = jax.ShapeDtypeStruct(
        (layers * (columns // parts) + level_room(layers), plane), jnp.bfloat16
    )
    return pl.pallas_call(
        functools.partial(split_kernel, bricks_y),
        in_specs=[pl.BlockSpec(memory_space=pltpu.HBM)] * 2,
        out_shape=[message] * parts,
        scratch_shapes=[
            pltpu.VMEM((columns, plane), jnp.float32),
            pltpu.VMEM((count, columns), jnp.bfloat16),
            pltpu.VMEM(potential.shape, jnp.float32),
            pltpu.SemaphoreType.DMA((layers + 1,)),
        ],
        compiler_params=pltpu.CompilerParams(vmem_limit_bytes=fetching_limit),
    )(cells, potential)


def place_kernel(bricks_y, *refs):
    parts = owned * bricks_y
    received_refs, results = refs[:parts], refs[parts:]
    edge_ref, inner_ref, edge_level_ref, inner_level_ref, own_ref, level_ref = results
    mid, y, core = lax.axis_index("mid"), lax.axis_index("gy"), lax.axis_index("core")
    rows = own_ref.shape[2]
    layers = level_ref.shape[2]
    for step, received_ref in zip(offsets(bricks_y), received_refs):
        at, b = behind(mid, y, step, bricks_y)
        own_ref[at, b] = received_ref[:rows]
        extra = received_ref[rows:].astype(jnp.float32)
        level = extra[:layers] + extra[layers : 2 * layers] + extra[2 * layers : 3 * layers]
        level_ref[at, b] = level
    edge_ref[...] = own_ref[core]
    inner_ref[...] = own_ref[1 - core]
    edge_level_ref[...] = level_ref[core]
    inner_level_ref[...] = level_ref[1 - core]


def place(received, layers, bricks_y):
    plane = received[0].shape[1]
    rows = received[0].shape[0] - level_room(layers)
    field = (bricks_y, rows, plane)
    level = (bricks_y, layers, plane)
    return pl.pallas_call(
        functools.partial(place_kernel, bricks_y),
        out_shape=[jax.ShapeDtypeStruct(field, jnp.bfloat16)] * 2
        + [jax.ShapeDtypeStruct(level, jnp.float32)] * 2,
        scratch_shapes=[
            pltpu.VMEM((owned,) + field, jnp.bfloat16),
            pltpu.VMEM((owned,) + level, jnp.float32),
        ],
        compiler_params=pltpu.CompilerParams(vmem_limit_bytes=vmem_limit),
    )(*received)


def plane_kernel(own_ref, level_ref, weights_ref, partial_ref):
    bricks_y, rows, plane = own_ref.shape
    layers = level_ref.shape[1]
    share = rows // layers
    for b in range(bricks_y):
        fields, weights = [], []
        for kind, other in ((0, b), (1, b - 1), (2, b + 1)):
            if 0 <= other < bricks_y:
                for part in range(weights_ref.shape[1]):
                    fields.append(own_ref[other])
                    weights.append(weights_ref[kind, part])
        sides = jnp.dot(
            jnp.concatenate(fields, axis=1),
            jnp.concatenate(weights, axis=0),
            preferred_element_type=jnp.float32,
        )
        for layer in range(layers):
            here = slice(layer * share, (layer + 1) * share)
            level = jnp.broadcast_to(level_ref[b, layer : layer + 1, :], (share, plane))
            partial_ref[b, here] = sides[here] + level * own_ref[b, here].astype(jnp.float32)


def plane_part(own, level, weights):
    bricks_y, rows, plane = own.shape
    flops = 2 * bricks_y * bricks_y * 3 * rows * plane * plane
    return pl.pallas_call(
        plane_kernel,
        out_shape=jax.ShapeDtypeStruct(own.shape, jnp.float32),
        cost_estimate=pl.CostEstimate(flops=flops, bytes_accessed=own.size * 6, transcendentals=0),
        compiler_params=pltpu.CompilerParams(vmem_limit_bytes=vmem_limit),
    )(own, level, weights)


def layer_kernel(first, layers, pack, partial_ref, own_ref, outer_ref, other_ref, *refs):
    refs = list(refs)
    before_ref = None if first else refs.pop(0)
    inner_ref = refs.pop(0) if pack else None
    next_ref = refs.pop()
    core, mid, y = lax.axis_index("core"), lax.axis_index("mid"), lax.axis_index("gy")
    bricks_y, rows, plane = own_ref.shape
    share = rows // layers
    width = min(plane, 128)

    def step(low_ref, high_ref):
        for b in range(bricks_y):
            for column in range(0, share, group):
                for left in range(0, plane, width):
                    lane = slice(left, left + width)
                    places = [
                        slice(layer * share + column, layer * share + column + group)
                        for layer in range(layers)
                    ]
                    window = [
                        ref[b, here, lane].astype(jnp.float32)
                        for ref in (low_ref, own_ref, high_ref)
                        for here in places
                    ]
                    for layer, here in enumerate(places):
                        value = partial_ref[b, here, lane]
                        for distance in range(1, stencil_reach + 1):
                            pair = window[layers + layer - distance] + window[layers + layer + distance]
                            value = value + side_weights[distance] * pair
                        if before_ref is not None:
                            value = 2.0 * value - before_ref[b, here, lane].astype(jnp.float32)
                        next_ref[b, here, lane] = value.astype(jnp.bfloat16)

    @pl.when(core == 0)
    def _():
        step(outer_ref, other_ref)

    @pl.when(core != 0)
    def _():
        step(other_ref, outer_ref)

    if pack:
        for offset, sent_ref in zip(offsets(bricks_y), refs):
            to_mid, to_y = ahead(mid, y, offset, bricks_y)

            @pl.when(to_mid == core)
            def _():
                sent_ref[...] = next_ref[to_y]

            @pl.when(to_mid != core)
            def _():
                sent_ref[...] = inner_ref[to_y]


def layer_part(layers, partial, own, outer, other, before, inner=None):
    bricks_y, rows, plane = own.shape
    pack = inner is not None
    operands = [partial, own, outer, other]
    operands += [] if before is None else [before]
    operands += [inner] if pack else []
    one = jax.ShapeDtypeStruct((rows, plane), jnp.bfloat16)
    return pl.pallas_call(
        functools.partial(layer_kernel, before is None, layers, pack),
        out_shape=[one] * (owned * bricks_y) if pack else jax.ShapeDtypeStruct(own.shape, jnp.bfloat16),
        scratch_shapes=[pltpu.VMEM(own.shape, jnp.bfloat16)] if pack else [],
        cost_estimate=pl.CostEstimate(
            flops=24 * own.size, bytes_accessed=own.size * 14, transcendentals=0
        ),
        compiler_params=pltpu.CompilerParams(vmem_limit_bytes=vmem_limit),
    )(*operands)


def from_other_core(own):
    return lax.ppermute(own, "core", [(0, 1), (1, 0)])


def from_next_chip(edge):
    count = lax.axis_size(("far", "core"))
    pairs = [(at, at + 1) for at in range(1, count - 1, 2)]
    return lax.ppermute(edge, ("far", "core"), pairs + [(b, a) for a, b in pairs])


def chebyshev(edge, inner, edge_level, inner_level, weights):
    layers = edge_level.shape[1]
    edge_before = inner_before = None
    for stage in range(DEG):
        outer = from_next_chip(edge)
        other_inner = from_other_core(inner)
        other_edge = from_other_core(edge)
        edge_partial = plane_part(edge, edge_level, weights)
        inner_partial = plane_part(inner, inner_level, weights)
        inner_next = layer_part(layers, inner_partial, inner, other_inner, other_edge, inner_before)
        last = inner_next if stage == DEG - 1 else None
        edge_next = layer_part(layers, edge_partial, edge, outer, other_inner, edge_before, last)
        edge_before, edge = edge, edge_next
        inner_before, inner = inner, inner_next
    return edge


def join_kernel(bricks_y, *refs):
    parts = owned * bricks_y
    received_refs, (cells_ref, gram_ref, block_ref) = refs[:parts], refs[parts:]
    mid, y = lax.axis_index("mid"), lax.axis_index("gy")
    columns, plane = block_ref.shape
    share = columns // parts
    layers = cells_ref.shape[0] // plane
    total = None
    for layer in range(layers):
        for step, received_ref in zip(offsets(bricks_y), received_refs):
            from_mid, from_y = behind(mid, y, step, bricks_y)
            first = pl.multiple_of((from_mid * bricks_y + from_y) * share, share)
            own = received_ref[layer * share : (layer + 1) * share, :]
            block_ref[pl.ds(first, share), :] = own.astype(jnp.float32)
        block = block_ref[...]
        cells_ref[layer * plane : (layer + 1) * plane, :] = block.T.astype(jnp.bfloat16)
        narrow = block.astype(jnp.bfloat16)
        part = lax.dot_general(
            narrow, narrow, (((1,), (1,)), ((), ())), preferred_element_type=jnp.float32
        )
        total = part if total is None else total + part
    half = columns // 2
    packed = jnp.concatenate([total[:half], total[half:, half:]], axis=1)
    piece = gram_ref.shape[1]
    for device in range(gram_ref.shape[0]):
        gram_ref[device] = packed[device * piece : (device + 1) * piece]


def join_columns(received, layers, bricks_y):
    rows, plane = received[0].shape
    columns = rows // layers * owned * bricks_y
    half = columns // 2
    shares = math.gcd(lax.axis_size(axes), half)
    return pl.pallas_call(
        functools.partial(join_kernel, bricks_y),
        out_shape=(
            jax.ShapeDtypeStruct((layers * plane, columns), jnp.bfloat16),
            jax.ShapeDtypeStruct((shares, half // shares, 3 * half), jnp.float32),
        ),
        scratch_shapes=[pltpu.VMEM((columns, plane), jnp.float32)],
        compiler_params=pltpu.CompilerParams(vmem_limit_bytes=vmem_limit),
    )(*received)


lanes = 128
panel_rows = 8
block_rows = 64


def row_splat(values, row):
    return jnp.broadcast_to(values[row : row + 1, :], values.shape)


def lane_splat(values, lane):
    return jnp.broadcast_to(values[:, lane : lane + 1], (panel_rows, lanes))


def panel_inverse(columns):
    row = lax.broadcasted_iota(jnp.int32, (panel_rows, lanes), 0)
    columns = list(columns)
    full = [jnp.where(row == k, 1.0, 0.0).astype(jnp.float32) for k in range(panel_rows)]
    forward = list(full)
    pivots = jnp.zeros((panel_rows, lanes), jnp.float32)
    for step in range(panel_rows):
        pivot = row_splat(columns[step], step)
        scale = 1.0 / pivot
        pivots = jnp.where(row == step, pivot, pivots)
        others = jnp.where(row == step, 0.0, columns[step])
        for k in range(step + 1, panel_rows):
            columns[k] = columns[k] - others * (row_splat(columns[k], step) * scale)
        for k in range(step):
            forward[k] = jnp.where(row == step, full[k], forward[k])
            full[k] = full[k] - others * (row_splat(full[k], step) * scale)
        full[step] = full[step] - others * scale
    inverse_pivots = 1.0 / pivots
    root = lax.rsqrt(pivots)
    full = [column * inverse_pivots for column in full]
    forward = [column * root for column in forward]
    return full, forward


def combine(columns, rows):
    width = rows.shape[1] // lanes
    parts = []
    for part in range(width):
        piece = rows[:, part * lanes : (part + 1) * lanes]
        total = None
        for k, column in enumerate(columns):
            term = column * row_splat(piece, k)
            total = term if total is None else total + term
        parts.append(total)
    return jnp.concatenate(parts, axis=1)


def factor_kernel(scale, gram_ref, rows_ref, rotated_ref, upper_ref, packed_ref, factor_ref, inverse_ref):
    shares, piece, width = gram_ref.shape
    half = shares * piece
    order = 2 * half
    for share in range(shares):
        packed_ref[share * piece : (share + 1) * piece, :] = gram_ref[share]
    factor_ref[...] = jnp.zeros((order, order), jnp.float32)
    inverse_ref[...] = jnp.zeros((order, order), jnp.float32)
    for start in range(0, order, block_rows):
        left = start // lanes * lanes
        right = left + lanes
        local = start - left
        row = lax.broadcasted_iota(jnp.int32, (block_rows, right), 0)
        col = lax.broadcasted_iota(jnp.int32, (block_rows, right), 1)
        unit = jnp.where(col == row + start, 1.0, 0.0).astype(jnp.float32)
        at, side = (start, 0) if start < half else (start - half, order)
        own = packed_ref[at : at + block_rows, side : side + order - left]
        block = jnp.concatenate([own, unit], axis=1)
        if start > 0:
            done = jnp.concatenate(
                [factor_ref[:start, left:order], inverse_ref[:start, :right]], axis=1
            )
            update = lax.dot_general(
                factor_ref[:start, left : left + lanes],
                done,
                (((0,), (0,)), ((), ())),
                precision=lax.Precision.HIGHEST,
                preferred_element_type=jnp.float32,
            )
            block = block - update[local : local + block_rows]
        groups = [
            block[g : g + panel_rows] for g in range(0, block_rows, panel_rows)
        ]
        for index in range(len(groups)):
            lane = local + index * panel_rows
            rows = groups[index]
            full, forward = panel_inverse([lane_splat(rows, lane + k) for k in range(panel_rows)])
            step_rows = combine(full, rows)
            for other in range(index + 1, len(groups)):
                target = groups[other]
                columns = [lane_splat(target, lane + k) for k in range(panel_rows)]
                groups[other] = target - combine(columns, step_rows)
            finished = combine(forward, rows)
            at = start + index * panel_rows
            factor_ref[at : at + panel_rows, left:order] = finished[:, : order - left]
            inverse_ref[at : at + panel_rows, :right] = finished[:, order - left :]
    row = lax.broadcasted_iota(jnp.int32, (order, order), 0)
    col = lax.broadcasted_iota(jnp.int32, (order, order), 1)
    upper_ref[...] = jnp.where(col >= row, factor_ref[...] * (1.0 / scale), 0.0)
    inverse = jnp.where(col <= row, inverse_ref[...] * scale, 0.0)
    high = inverse.astype(jnp.bfloat16)
    rest = inverse - high.astype(jnp.float32)
    middle = rest.astype(jnp.bfloat16)
    low = (rest - middle.astype(jnp.float32)).astype(jnp.bfloat16)
    count = rows_ref.shape[0]
    chunk = math.gcd(count, 512)
    for at in range(0, count, chunk):
        piece = rows_ref[at : at + chunk, :]
        total = jnp.zeros((chunk, order), jnp.float32)
        for part in (low, middle, high):
            total = total + lax.dot_general(
                piece, part, (((1,), (1,)), ((), ())), preferred_element_type=jnp.float32
            )
        rotated_ref[at : at + chunk, :] = total.astype(jnp.bfloat16)


def factor_and_rotate(gram_matrix, rows, total_cells):
    order = rows.shape[1]
    count = rows.shape[0]
    return pl.pallas_call(
        functools.partial(factor_kernel, math.sqrt(total_cells)),
        out_shape=(
            jax.ShapeDtypeStruct((count, order), jnp.bfloat16),
            jax.ShapeDtypeStruct((order, order), jnp.float32),
        ),
        scratch_shapes=[
            pltpu.VMEM((order // 2, order // 2 * 3), jnp.float32),
            pltpu.VMEM((order, order), jnp.float32),
            pltpu.VMEM((order, order), jnp.float32),
        ],
        compiler_params=pltpu.CompilerParams(vmem_limit_bytes=vmem_limit),
    )(gram_matrix, rows)


def sum_over_devices(values):
    if lax.axis_size(axes) != values.shape[0]:
        return lax.psum(values, axes)
    total = jnp.sum(lax.all_to_all(values, axes, 0, 0), axis=0)
    return lax.all_to_all(jnp.broadcast_to(total[None], values.shape), axes, 0, 0)


def shards(trial_orbitals, potential):
    layers, extent_y, extent_z, columns = trial_orbitals.shape
    bricks_y = lax.axis_size("gy")
    total_cells = lax.axis_size(axes) * layers * extent_y * extent_z
    weights = jnp.asarray(plane_weights(extent_y, extent_z))

    cells = trial_orbitals.reshape(layers * extent_y * extent_z, columns)
    sent = split_columns(cells, potential, bricks_y)
    placed = place(exchange(sent, bricks_y), layers, bricks_y)
    sent = chebyshev(*placed, weights)
    rows, local_gram = join_columns(exchange(sent, bricks_y), layers, bricks_y)
    gram_matrix = sum_over_devices(local_gram)
    rotated, upper_factor = factor_and_rotate(gram_matrix, rows, total_cells)
    return (rotated.reshape(trial_orbitals.shape), upper_factor)


def solution(mesh):
    bricks_x, bricks_y = mesh.devices.shape
    cut = Mesh(mesh.devices.reshape(bricks_x // 4, owned, 2, bricks_y), axes)
    cells = P(("far", "mid", "core"), "gy")
    return jax.shard_map(
        shards,
        mesh=cut,
        in_specs=(cells, cells),
        out_specs=(cells, P()),
        check_vma=False,
    )
```

```python
import functools
import math

import jax
import jax.numpy as jnp
import ml_dtypes
import numpy as np
from jax import lax
from jax.experimental import pallas as pl
from jax.experimental.pallas import tpu as pltpu
from jax.sharding import Mesh, PartitionSpec as P

DEG = 3


STENCIL_WEIGHTS = (
    -5369.0 / 1800.0,
    12.0 / 7.0,
    -15.0 / 56.0,
    10.0 / 189.0,
    -1.0 / 112.0,
    2.0 / 1925.0,
    -1.0 / 16632.0,
)
stencil_reach = 6
filter_center = 11.5
filter_half = 8.5
axes = ("far", "mid", "core", "gy")
owned = 2
group = 16
vmem_limit = 48 * 1024 * 1024

center_shift = -1.5 * STENCIL_WEIGHTS[0] - filter_center
side_weights = tuple(-0.5 * weight / filter_half for weight in STENCIL_WEIGHTS)


def bfloat16_parts(values):
    parts = []
    rest = np.asarray(values, np.float32)
    for _ in range(3):
        part = rest.astype(ml_dtypes.bfloat16)
        parts.append(part)
        rest = rest - part.astype(np.float32)
    return np.stack(parts)


def plane_weights(extent_y, extent_z):
    def band(extent, shift):
        matrix = np.zeros((extent, extent), np.float64)
        for source in range(extent):
            for target in range(extent):
                distance = abs(target - (source + shift))
                if 1 <= distance <= stencil_reach:
                    matrix[source, target] = side_weights[distance]
        return matrix

    eye_y, eye_z = np.eye(extent_y), np.eye(extent_z)
    own = np.kron(band(extent_y, 0), eye_z) + np.kron(eye_y, band(extent_z, 0))
    before = np.kron(band(extent_y, -extent_y), eye_z)
    after = np.kron(band(extent_y, extent_y), eye_z)
    return np.stack([bfloat16_parts(part) for part in (own, before, after)])


def level_rows(potential, rows):
    rest = (potential + center_shift) * (1.0 / filter_half)
    parts = []
    for _ in range(3):
        part = rest.astype(jnp.bfloat16).astype(jnp.float32)
        parts.append(part)
        rest = rest - part
    unused = jnp.zeros((rows - 3 * rest.shape[0], rest.shape[1]), jnp.float32)
    return jnp.concatenate(parts + [unused], axis=0).astype(jnp.bfloat16)


def level_room(layers):
    return -(-3 * layers // 16) * 16


def offsets(bricks_y):
    return [(i, j) for i in range(owned) for j in range(bricks_y)]


def ahead(mid, y, step, bricks_y):
    return lax.rem(mid + step[0], owned), lax.rem(y + step[1], bricks_y)


def behind(mid, y, step, bricks_y):
    return lax.rem(mid + step[0], owned), lax.rem(y - step[1] + bricks_y, bricks_y)


def exchange(messages, bricks_y):
    result = [messages[0]]
    for step, message in list(zip(offsets(bricks_y), messages))[1:]:
        perm = []
        for mid in range(owned):
            for y in range(bricks_y):
                target = (mid + step[0]) % owned * bricks_y + (y + step[1]) % bricks_y
                perm.append((mid * bricks_y + y, target))
        result.append(lax.ppermute(message, ("mid", "gy"), perm))
    return result


def split_kernel(bricks_y, cells_ref, potential_ref, *refs):
    sent_refs, block_ref = refs[:-1], refs[-1]
    mid, y = lax.axis_index("mid"), lax.axis_index("gy")
    columns, plane = block_ref.shape
    share = columns // len(sent_refs)
    layers = cells_ref.shape[0] // plane
    potential = jnp.concatenate(
        [potential_ref[:, at, :] for at in range(potential_ref.shape[1])], axis=1
    )
    extra = level_rows(potential, sent_refs[0].shape[0] - layers * share)
    for sent_ref in sent_refs:
        sent_ref[layers * share :, :] = extra
    for layer in range(layers):
        block = cells_ref[layer * plane : (layer + 1) * plane, :].astype(jnp.float32)
        block_ref[...] = block.T
        for step, sent_ref in zip(offsets(bricks_y), sent_refs):
            to_mid, to_y = ahead(mid, y, step, bricks_y)
            first = pl.multiple_of((to_mid * bricks_y + to_y) * share, share)
            own = block_ref[pl.ds(first, share), :]
            sent_ref[layer * share : (layer + 1) * share, :] = own.astype(jnp.bfloat16)


def split_columns(cells, potential, bricks_y):
    count, columns = cells.shape
    layers = potential.shape[0]
    plane = count // layers
    parts = owned * bricks_y
    message = jax.ShapeDtypeStruct(
        (layers * (columns // parts) + level_room(layers), plane), jnp.bfloat16
    )
    return pl.pallas_call(
        functools.partial(split_kernel, bricks_y),
        out_shape=[message] * parts,
        scratch_shapes=[pltpu.VMEM((columns, plane), jnp.float32)],
        compiler_params=pltpu.CompilerParams(vmem_limit_bytes=vmem_limit),
    )(cells, potential)


def taker(refs, bricks_y):
    rest = iter(refs)
    return lambda count=bricks_y: [next(rest) for _ in range(count)]


def place_kernel(bricks_y, *refs):
    take = taker(refs, bricks_y)
    received_refs = take(owned * bricks_y)
    edge_refs, inner_refs = take(), take()
    edge_level_ref, inner_level_ref, own_ref, level_ref = take(4)
    mid, y, core = lax.axis_index("mid"), lax.axis_index("gy"), lax.axis_index("core")
    rows = own_ref.shape[2]
    layers = level_ref.shape[2]
    for step, received_ref in zip(offsets(bricks_y), received_refs):
        at, b = behind(mid, y, step, bricks_y)
        own_ref[at, b] = received_ref[:rows]
        extra = received_ref[rows:].astype(jnp.float32)
        level = extra[:layers] + extra[layers : 2 * layers] + extra[2 * layers : 3 * layers]
        level_ref[at, b] = level
    for b in range(bricks_y):
        edge_refs[b][...] = own_ref[core, b]
        inner_refs[b][...] = own_ref[1 - core, b]
    edge_level_ref[...] = level_ref[core]
    inner_level_ref[...] = level_ref[1 - core]


def place(received, layers, bricks_y):
    plane = received[0].shape[1]
    rows = received[0].shape[0] - level_room(layers)
    field = (rows, plane)
    level = (bricks_y, layers, plane)
    results = pl.pallas_call(
        functools.partial(place_kernel, bricks_y),
        out_shape=[jax.ShapeDtypeStruct(field, jnp.bfloat16)] * (2 * bricks_y)
        + [jax.ShapeDtypeStruct(level, jnp.float32)] * 2,
        scratch_shapes=[
            pltpu.VMEM((owned, bricks_y) + field, jnp.bfloat16),
            pltpu.VMEM((owned,) + level, jnp.float32),
        ],
        compiler_params=pltpu.CompilerParams(vmem_limit_bytes=vmem_limit),
    )(*received)
    return results[:bricks_y], results[bricks_y : 2 * bricks_y], results[-2], results[-1]


def plane_kernel(bricks_y, *refs):
    take = taker(refs, bricks_y)
    own_refs, (level_ref, weights_ref), partial_refs = take(), take(2), take()
    rows, plane = own_refs[0].shape
    layers = level_ref.shape[1]
    share = rows // layers
    for b in range(bricks_y):
        fields, weights = [], []
        for kind, other in ((0, b), (1, b - 1), (2, b + 1)):
            if 0 <= other < bricks_y:
                for part in range(weights_ref.shape[1]):
                    fields.append(own_refs[other][...])
                    weights.append(weights_ref[kind, part])
        sides = jnp.dot(
            jnp.concatenate(fields, axis=1),
            jnp.concatenate(weights, axis=0),
            preferred_element_type=jnp.float32,
        )
        for layer in range(layers):
            here = slice(layer * share, (layer + 1) * share)
            level = jnp.broadcast_to(level_ref[b, layer : layer + 1, :], (share, plane))
            partial_refs[b][here] = sides[here] + level * own_refs[b][here].astype(jnp.float32)


def plane_part(own, level, weights):
    bricks_y = len(own)
    rows, plane = own[0].shape
    flops = 2 * bricks_y * bricks_y * 3 * rows * plane * plane
    return pl.pallas_call(
        functools.partial(plane_kernel, bricks_y),
        out_shape=[jax.ShapeDtypeStruct((rows, plane), jnp.float32)] * bricks_y,
        cost_estimate=pl.CostEstimate(
            flops=flops, bytes_accessed=6 * bricks_y * rows * plane, transcendentals=0
        ),
        compiler_params=pltpu.CompilerParams(vmem_limit_bytes=vmem_limit),
    )(*own, level, weights)


def layer_kernel(first, layers, bricks_y, pack, *refs):
    take = taker(refs, bricks_y)
    partial_refs, own_refs, outer_refs, other_refs = take(), take(), take(), take()
    before_refs = None if first else take()
    inner_refs = take() if pack else None
    sent_refs = take(owned * bricks_y) if pack else None
    next_refs = take()
    core, mid, y = lax.axis_index("core"), lax.axis_index("mid"), lax.axis_index("gy")
    rows, plane = own_refs[0].shape
    share = rows // layers
    width = min(plane, 128)

    def step(low_refs, high_refs):
        for b in range(bricks_y):
            for column in range(0, share, group):
                for left in range(0, plane, width):
                    lane = slice(left, left + width)
                    places = [
                        slice(layer * share + column, layer * share + column + group)
                        for layer in range(layers)
                    ]
                    window = [
                        ref[here, lane].astype(jnp.float32)
                        for ref in (low_refs[b], own_refs[b], high_refs[b])
                        for here in places
                    ]
                    for layer, here in enumerate(places):
                        value = partial_refs[b][here, lane]
                        for distance in range(1, stencil_reach + 1):
                            pair = window[layers + layer - distance] + window[layers + layer + distance]
                            value = value + side_weights[distance] * pair
                        if before_refs is not None:
                            value = 2.0 * value - before_refs[b][here, lane].astype(jnp.float32)
                        next_refs[b][here, lane] = value.astype(jnp.bfloat16)

    @pl.when(core == 0)
    def _():
        step(outer_refs, other_refs)

    @pl.when(core != 0)
    def _():
        step(other_refs, outer_refs)

    if pack:
        for offset, sent_ref in zip(offsets(bricks_y), sent_refs):
            to_mid, to_y = ahead(mid, y, offset, bricks_y)
            for b in range(bricks_y):

                @pl.when((to_mid == core) & (to_y == b))
                def _():
                    sent_ref[...] = next_refs[b][...]

                @pl.when((to_mid != core) & (to_y == b))
                def _():
                    sent_ref[...] = inner_refs[b][...]


def layer_part(layers, partial, own, outer, other, before, inner=None):
    bricks_y = len(own)
    rows, plane = own[0].shape
    pack = inner is not None
    operands = [*partial, *own, *outer, *other, *(before or []), *(inner or [])]
    size = bricks_y * rows * plane
    one = jax.ShapeDtypeStruct((rows, plane), jnp.bfloat16)
    return pl.pallas_call(
        functools.partial(layer_kernel, before is None, layers, bricks_y, pack),
        out_shape=[one] * (owned * bricks_y if pack else bricks_y),
        scratch_shapes=[pltpu.VMEM((rows, plane), jnp.bfloat16)] * bricks_y if pack else [],
        cost_estimate=pl.CostEstimate(flops=24 * size, bytes_accessed=14 * size, transcendentals=0),
        compiler_params=pltpu.CompilerParams(vmem_limit_bytes=vmem_limit),
    )(*operands)


def from_other_core(own):
    return [lax.ppermute(brick, "core", [(0, 1), (1, 0)]) for brick in own]


def from_next_chip(edge):
    count = lax.axis_size(("far", "core"))
    pairs = [(at, at + 1) for at in range(1, count - 1, 2)]
    both = pairs + [(b, a) for a, b in pairs]
    return [lax.ppermute(brick, ("far", "core"), both) for brick in edge]


def chebyshev(edge, inner, edge_level, inner_level, weights):
    layers = edge_level.shape[1]
    edge_before = inner_before = None
    for stage in range(DEG):
        outer = from_next_chip(edge)
        other_inner = from_other_core(inner)
        other_edge = from_other_core(edge)
        edge_partial = plane_part(edge, edge_level, weights)
        inner_partial = plane_part(inner, inner_level, weights)
        inner_next = layer_part(layers, inner_partial, inner, other_inner, other_edge, inner_before)
        last = inner_next if stage == DEG - 1 else None
        edge_next = layer_part(layers, edge_partial, edge, outer, other_inner, edge_before, last)
        edge_before, edge = edge, edge_next
        inner_before, inner = inner, inner_next
    return edge


def join_kernel(bricks_y, *refs):
    parts = owned * bricks_y
    received_refs, (cells_ref, gram_ref, block_ref) = refs[:parts], refs[parts:]
    mid, y = lax.axis_index("mid"), lax.axis_index("gy")
    columns, plane = block_ref.shape
    share = columns // parts
    layers = cells_ref.shape[0] // plane
    total = None
    for layer in range(layers):
        for step, received_ref in zip(offsets(bricks_y), received_refs):
            from_mid, from_y = behind(mid, y, step, bricks_y)
            first = pl.multiple_of((from_mid * bricks_y + from_y) * share, share)
            own = received_ref[layer * share : (layer + 1) * share, :]
            block_ref[pl.ds(first, share), :] = own.astype(jnp.float32)
        block = block_ref[...]
        cells_ref[layer * plane : (layer + 1) * plane, :] = block.T.astype(jnp.bfloat16)
        narrow = block.astype(jnp.bfloat16)
        part = lax.dot_general(
            narrow, narrow, (((1,), (1,)), ((), ())), preferred_element_type=jnp.float32
        )
        total = part if total is None else total + part
    half = columns // 2
    packed = jnp.concatenate([total[:half], total[half:, half:]], axis=1)
    piece = gram_ref.shape[1]
    for device in range(gram_ref.shape[0]):
        gram_ref[device] = packed[device * piece : (device + 1) * piece]


def join_columns(received, layers, bricks_y):
    rows, plane = received[0].shape
    columns = rows // layers * owned * bricks_y
    half = columns // 2
    shares = math.gcd(lax.axis_size(axes), half)
    return pl.pallas_call(
        functools.partial(join_kernel, bricks_y),
        out_shape=(
            jax.ShapeDtypeStruct((layers * plane, columns), jnp.bfloat16),
            jax.ShapeDtypeStruct((shares, half // shares, 3 * half), jnp.float32),
        ),
        scratch_shapes=[pltpu.VMEM((columns, plane), jnp.float32)],
        compiler_params=pltpu.CompilerParams(vmem_limit_bytes=vmem_limit),
    )(*received)


lanes = 128
panel_rows = 8
block_rows = 64


def row_splat(values, row):
    return jnp.broadcast_to(values[row : row + 1, :], values.shape)


def lane_splat(values, lane):
    return jnp.broadcast_to(values[:, lane : lane + 1], (panel_rows, lanes))


def panel_inverse(columns):
    row = lax.broadcasted_iota(jnp.int32, (panel_rows, lanes), 0)
    columns = list(columns)
    full = [jnp.where(row == k, 1.0, 0.0).astype(jnp.float32) for k in range(panel_rows)]
    forward = list(full)
    scales = jnp.zeros((panel_rows, lanes), jnp.float32)
    for step in range(panel_rows):
        scale = 1.0 / row_splat(columns[step], step)
        scales = jnp.where(row == step, scale, scales)
        others = jnp.where(row == step, 0.0, columns[step])
        for k in range(step + 1, panel_rows):
            columns[k] = columns[k] - others * (row_splat(columns[k], step) * scale)
        for k in range(step):
            forward[k] = jnp.where(row == step, full[k], forward[k])
            full[k] = full[k] - others * (row_splat(full[k], step) * scale)
        full[step] = full[step] - others * scale
    root = jnp.sqrt(scales)
    full = [column * scales for column in full]
    forward = [column * root for column in forward]
    return full, forward


def combine(columns, rows):
    parts = []
    for left in range(0, rows.shape[1], lanes):
        piece = rows[:, left : left + lanes]
        terms = [column * row_splat(piece, k) for k, column in enumerate(columns)]
        while len(terms) > 1:
            terms = [a + b for a, b in zip(terms[::2], terms[1::2])]
        parts.append(terms[0])
    return jnp.concatenate(parts, axis=1)


def factor_kernel(scale, gram_ref, rows_ref, rotated_ref, upper_ref, packed_ref, factor_ref, inverse_ref):
    shares, piece, width = gram_ref.shape
    half = shares * piece
    order = 2 * half
    for share in range(shares):
        packed_ref[share * piece : (share + 1) * piece, :] = gram_ref[share]
    factor_ref[...] = jnp.zeros((order, order), jnp.float32)
    inverse_ref[...] = jnp.zeros((order, order), jnp.float32)
    for start in range(0, order, block_rows):
        left = start // lanes * lanes
        right = left + lanes
        local = start - left
        row = lax.broadcasted_iota(jnp.int32, (block_rows, right), 0)
        col = lax.broadcasted_iota(jnp.int32, (block_rows, right), 1)
        unit = jnp.where(col == row + start, 1.0, 0.0).astype(jnp.float32)
        at, side = (start, 0) if start < half else (start - half, order)
        own = packed_ref[at : at + block_rows, side : side + order - left]
        block = jnp.concatenate([own, unit], axis=1)
        if start > 0:
            done = jnp.concatenate(
                [factor_ref[:start, left:order], inverse_ref[:start, :right]], axis=1
            )
            update = lax.dot_general(
                factor_ref[:start, left : left + lanes],
                done,
                (((0,), (0,)), ((), ())),
                precision=lax.Precision.HIGHEST,
                preferred_element_type=jnp.float32,
            )
            block = block - update[local : local + block_rows]
        groups = [
            block[g : g + panel_rows] for g in range(0, block_rows, panel_rows)
        ]
        for index in range(len(groups)):
            lane = local + index * panel_rows
            rows = groups[index]
            full, forward = panel_inverse([lane_splat(rows, lane + k) for k in range(panel_rows)])
            step_rows = combine(full, rows)
            for other in range(index + 1, len(groups)):
                target = groups[other]
                columns = [lane_splat(target, lane + k) for k in range(panel_rows)]
                groups[other] = target - combine(columns, step_rows)
            finished = combine(forward, rows)
            at = start + index * panel_rows
            factor_ref[at : at + panel_rows, left:order] = finished[:, : order - left]
            inverse_ref[at : at + panel_rows, :right] = finished[:, order - left :]
    row = lax.broadcasted_iota(jnp.int32, (order, order), 0)
    col = lax.broadcasted_iota(jnp.int32, (order, order), 1)
    upper_ref[...] = jnp.where(col >= row, factor_ref[...] * (1.0 / scale), 0.0)
    inverse = jnp.where(col <= row, inverse_ref[...] * scale, 0.0)
    high = inverse.astype(jnp.bfloat16)
    rest = inverse - high.astype(jnp.float32)
    middle = rest.astype(jnp.bfloat16)
    low = (rest - middle.astype(jnp.float32)).astype(jnp.bfloat16)
    count = rows_ref.shape[0]
    chunk = math.gcd(count, 512)
    for at in range(0, count, chunk):
        piece = rows_ref[at : at + chunk, :]
        total = jnp.zeros((chunk, order), jnp.float32)
        for part in (low, middle, high):
            total = total + lax.dot_general(
                piece, part, (((1,), (1,)), ((), ())), preferred_element_type=jnp.float32
            )
        rotated_ref[at : at + chunk, :] = total.astype(jnp.bfloat16)


def factor_and_rotate(gram_matrix, rows, total_cells):
    order = rows.shape[1]
    count = rows.shape[0]
    return pl.pallas_call(
        functools.partial(factor_kernel, math.sqrt(total_cells)),
        out_shape=(
            jax.ShapeDtypeStruct((count, order), jnp.bfloat16),
            jax.ShapeDtypeStruct((order, order), jnp.float32),
        ),
        scratch_shapes=[
            pltpu.VMEM((order // 2, order // 2 * 3), jnp.float32),
            pltpu.VMEM((order, order), jnp.float32),
            pltpu.VMEM((order, order), jnp.float32),
        ],
        compiler_params=pltpu.CompilerParams(vmem_limit_bytes=vmem_limit),
    )(gram_matrix, rows)


def sum_over_devices(values):
    if lax.axis_size(axes) != values.shape[0]:
        return lax.psum(values, axes)
    total = jnp.sum(lax.all_to_all(values, axes, 0, 0), axis=0)
    return lax.all_to_all(jnp.broadcast_to(total[None], values.shape), axes, 0, 0)


def shards(trial_orbitals, potential):
    layers, extent_y, extent_z, columns = trial_orbitals.shape
    bricks_y = lax.axis_size("gy")
    total_cells = lax.axis_size(axes) * layers * extent_y * extent_z
    weights = jnp.asarray(plane_weights(extent_y, extent_z))

    cells = trial_orbitals.reshape(layers * extent_y * extent_z, columns)
    sent = split_columns(cells, potential, bricks_y)
    placed = place(exchange(sent, bricks_y), layers, bricks_y)
    sent = chebyshev(*placed, weights)
    rows, local_gram = join_columns(exchange(sent, bricks_y), layers, bricks_y)
    gram_matrix = sum_over_devices(local_gram)
    rotated, upper_factor = factor_and_rotate(gram_matrix, rows, total_cells)
    return (rotated.reshape(trial_orbitals.shape), upper_factor)


def solution(mesh):
    bricks_x, bricks_y = mesh.devices.shape
    cut = Mesh(mesh.devices.reshape(bricks_x // 4, owned, 2, bricks_y), axes)
    cells = P(("far", "mid", "core"), "gy")
    return jax.shard_map(
        shards,
        mesh=cut,
        in_specs=(cells, cells),
        out_specs=(cells, P()),
        check_vma=False,
    )
```

```python
import functools
import math

import jax
import jax.numpy as jnp
import ml_dtypes
import numpy as np
from jax import lax
from jax.experimental import pallas as pl
from jax.experimental.pallas import tpu as pltpu
from jax.sharding import Mesh, PartitionSpec as P

DEG = 3


STENCIL_WEIGHTS = (
    -5369.0 / 1800.0,
    12.0 / 7.0,
    -15.0 / 56.0,
    10.0 / 189.0,
    -1.0 / 112.0,
    2.0 / 1925.0,
    -1.0 / 16632.0,
)
stencil_reach = 6
filter_center = 11.5
filter_half = 8.5
axes = ("far", "mid", "core", "gy")
owned = 2
group = 16
vmem_limit = 48 * 1024 * 1024

center_shift = -1.5 * STENCIL_WEIGHTS[0] - filter_center
side_weights = tuple(-0.5 * weight / filter_half for weight in STENCIL_WEIGHTS)


def bfloat16_parts(values):
    parts = []
    rest = np.asarray(values, np.float32)
    for _ in range(3):
        part = rest.astype(ml_dtypes.bfloat16)
        parts.append(part)
        rest = rest - part.astype(np.float32)
    return np.stack(parts)


def plane_weights(extent_y, extent_z):
    def band(extent, shift):
        matrix = np.zeros((extent, extent), np.float64)
        for source in range(extent):
            for target in range(extent):
                distance = abs(target - (source + shift))
                if 1 <= distance <= stencil_reach:
                    matrix[source, target] = side_weights[distance]
        return matrix

    eye_y, eye_z = np.eye(extent_y), np.eye(extent_z)
    own = np.kron(band(extent_y, 0), eye_z) + np.kron(eye_y, band(extent_z, 0))
    before = np.kron(band(extent_y, -extent_y), eye_z)
    after = np.kron(band(extent_y, extent_y), eye_z)
    return np.stack([bfloat16_parts(part) for part in (own, before, after)])


def level_rows(potential, rows):
    rest = (potential + center_shift) * (1.0 / filter_half)
    parts = []
    for _ in range(3):
        part = rest.astype(jnp.bfloat16).astype(jnp.float32)
        parts.append(part)
        rest = rest - part
    unused = jnp.zeros((rows - 3 * rest.shape[0], rest.shape[1]), jnp.float32)
    return jnp.concatenate(parts + [unused], axis=0).astype(jnp.bfloat16)


def level_room(layers):
    return -(-3 * layers // 16) * 16


def offsets(bricks_y):
    return [(i, j) for i in range(owned) for j in range(bricks_y)]


def ahead(mid, y, step, bricks_y):
    return lax.rem(mid + step[0], owned), lax.rem(y + step[1], bricks_y)


def behind(mid, y, step, bricks_y):
    return lax.rem(mid + step[0], owned), lax.rem(y - step[1] + bricks_y, bricks_y)


def exchange(messages, bricks_y):
    result = [messages[0]]
    for step, message in list(zip(offsets(bricks_y), messages))[1:]:
        perm = []
        for mid in range(owned):
            for y in range(bricks_y):
                target = (mid + step[0]) % owned * bricks_y + (y + step[1]) % bricks_y
                perm.append((mid * bricks_y + y, target))
        result.append(lax.ppermute(message, ("mid", "gy"), perm))
    return result


def split_kernel(bricks_y, cells_ref, potential_ref, *refs):
    sent_refs, block_ref = refs[:-1], refs[-1]
    mid, y = lax.axis_index("mid"), lax.axis_index("gy")
    columns, plane = block_ref.shape
    share = columns // len(sent_refs)
    layers = cells_ref.shape[0] // plane
    potential = jnp.concatenate(
        [potential_ref[:, at, :] for at in range(potential_ref.shape[1])], axis=1
    )
    extra = level_rows(potential, sent_refs[0].shape[0] - layers * share)
    for sent_ref in sent_refs:
        sent_ref[layers * share :, :] = extra
    for layer in range(layers):
        block = cells_ref[layer * plane : (layer + 1) * plane, :].astype(jnp.float32)
        block_ref[...] = block.T
        for step, sent_ref in zip(offsets(bricks_y), sent_refs):
            to_mid, to_y = ahead(mid, y, step, bricks_y)
            first = pl.multiple_of((to_mid * bricks_y + to_y) * share, share)
            own = block_ref[pl.ds(first, share), :]
            sent_ref[layer * share : (layer + 1) * share, :] = own.astype(jnp.bfloat16)


def split_columns(cells, potential, bricks_y):
    count, columns = cells.shape
    layers = potential.shape[0]
    plane = count // layers
    parts = owned * bricks_y
    message = jax.ShapeDtypeStruct(
        (layers * (columns // parts) + level_room(layers), plane), jnp.bfloat16
    )
    return pl.pallas_call(
        functools.partial(split_kernel, bricks_y),
        out_shape=[message] * parts,
        scratch_shapes=[pltpu.VMEM((columns, plane), jnp.float32)],
        compiler_params=pltpu.CompilerParams(vmem_limit_bytes=vmem_limit),
    )(cells, potential)


def place_kernel(bricks_y, *refs):
    parts = owned * bricks_y
    received_refs, results = refs[:parts], refs[parts:]
    edge_ref, inner_ref, edge_level_ref, inner_level_ref, own_ref, level_ref = results
    mid, y, core = lax.axis_index("mid"), lax.axis_index("gy"), lax.axis_index("core")
    rows = own_ref.shape[2]
    layers = level_ref.shape[2]
    for step, received_ref in zip(offsets(bricks_y), received_refs):
        at, b = behind(mid, y, step, bricks_y)
        own_ref[at, b] = received_ref[:rows]
        extra = received_ref[rows:].astype(jnp.float32)
        level = extra[:layers] + extra[layers : 2 * layers] + extra[2 * layers : 3 * layers]
        level_ref[at, b] = level
    edge_ref[...] = own_ref[core]
    inner_ref[...] = own_ref[1 - core]
    edge_level_ref[...] = level_ref[core]
    inner_level_ref[...] = level_ref[1 - core]


def place(received, layers, bricks_y):
    plane = received[0].shape[1]
    rows = received[0].shape[0] - level_room(layers)
    field = (bricks_y, rows, plane)
    level = (bricks_y, layers, plane)
    return pl.pallas_call(
        functools.partial(place_kernel, bricks_y),
        out_shape=[jax.ShapeDtypeStruct(field, jnp.bfloat16)] * 2
        + [jax.ShapeDtypeStruct(level, jnp.float32)] * 2,
        scratch_shapes=[
            pltpu.VMEM((owned,) + field, jnp.bfloat16),
            pltpu.VMEM((owned,) + level, jnp.float32),
        ],
        compiler_params=pltpu.CompilerParams(vmem_limit_bytes=vmem_limit),
    )(*received)


def plane_kernel(own_ref, level_ref, weights_ref, partial_ref):
    bricks_y, rows, plane = own_ref.shape
    layers = level_ref.shape[1]
    share = rows // layers
    for b in range(bricks_y):
        fields, weights = [], []
        for kind, other in ((0, b), (1, b - 1), (2, b + 1)):
            if 0 <= other < bricks_y:
                for part in range(weights_ref.shape[1]):
                    fields.append(own_ref[other])
                    weights.append(weights_ref[kind, part])
        sides = jnp.dot(
            jnp.concatenate(fields, axis=1),
            jnp.concatenate(weights, axis=0),
            preferred_element_type=jnp.float32,
        )
        for layer in range(layers):
            here = slice(layer * share, (layer + 1) * share)
            level = jnp.broadcast_to(level_ref[b, layer : layer + 1, :], (share, plane))
            partial_ref[b, here] = sides[here] + level * own_ref[b, here].astype(jnp.float32)


def plane_part(own, level, weights):
    bricks_y, rows, plane = own.shape
    flops = 2 * bricks_y * bricks_y * 3 * rows * plane * plane
    return pl.pallas_call(
        plane_kernel,
        out_shape=jax.ShapeDtypeStruct(own.shape, jnp.float32),
        cost_estimate=pl.CostEstimate(flops=flops, bytes_accessed=own.size * 6, transcendentals=0),
        compiler_params=pltpu.CompilerParams(vmem_limit_bytes=vmem_limit),
    )(own, level, weights)


def layer_kernel(first, layers, pack, partial_ref, own_ref, outer_ref, other_ref, *refs):
    refs = list(refs)
    before_ref = None if first else refs.pop(0)
    inner_ref = refs.pop(0) if pack else None
    next_ref = refs.pop()
    core, mid, y = lax.axis_index("core"), lax.axis_index("mid"), lax.axis_index("gy")
    bricks_y, rows, plane = own_ref.shape
    share = rows // layers
    width = min(plane, 128)

    def step(low_ref, high_ref):
        for b in range(bricks_y):
            for column in range(0, share, group):
                for left in range(0, plane, width):
                    lane = slice(left, left + width)
                    places = [
                        slice(layer * share + column, layer * share + column + group)
                        for layer in range(layers)
                    ]
                    window = [
                        ref[b, here, lane].astype(jnp.float32)
                        for ref in (low_ref, own_ref, high_ref)
                        for here in places
                    ]
                    for layer, here in enumerate(places):
                        value = partial_ref[b, here, lane]
                        for distance in range(1, stencil_reach + 1):
                            pair = window[layers + layer - distance] + window[layers + layer + distance]
                            value = value + side_weights[distance] * pair
                        if before_ref is not None:
                            value = 2.0 * value - before_ref[b, here, lane].astype(jnp.float32)
                        next_ref[b, here, lane] = value.astype(jnp.bfloat16)

    @pl.when(core == 0)
    def _():
        step(outer_ref, other_ref)

    @pl.when(core != 0)
    def _():
        step(other_ref, outer_ref)

    if pack:
        for offset, sent_ref in zip(offsets(bricks_y), refs):
            to_mid, to_y = ahead(mid, y, offset, bricks_y)

            @pl.when(to_mid == core)
            def _():
                sent_ref[...] = next_ref[to_y]

            @pl.when(to_mid != core)
            def _():
                sent_ref[...] = inner_ref[to_y]


def layer_part(layers, partial, own, outer, other, before, inner=None):
    bricks_y, rows, plane = own.shape
    pack = inner is not None
    operands = [partial, own, outer, other]
    operands += [] if before is None else [before]
    operands += [inner] if pack else []
    one = jax.ShapeDtypeStruct((rows, plane), jnp.bfloat16)
    return pl.pallas_call(
        functools.partial(layer_kernel, before is None, layers, pack),
        out_shape=[one] * (owned * bricks_y) if pack else jax.ShapeDtypeStruct(own.shape, jnp.bfloat16),
        scratch_shapes=[pltpu.VMEM(own.shape, jnp.bfloat16)] if pack else [],
        cost_estimate=pl.CostEstimate(
            flops=24 * own.size, bytes_accessed=own.size * 14, transcendentals=0
        ),
        compiler_params=pltpu.CompilerParams(vmem_limit_bytes=vmem_limit),
    )(*operands)


def from_other_core(own):
    return lax.ppermute(own, "core", [(0, 1), (1, 0)])


def from_next_chip(edge):
    count = lax.axis_size(("far", "core"))
    pairs = [(at, at + 1) for at in range(1, count - 1, 2)]
    return lax.ppermute(edge, ("far", "core"), pairs + [(b, a) for a, b in pairs])


def chebyshev(edge, inner, edge_level, inner_level, weights):
    layers = edge_level.shape[1]
    edge_before = inner_before = None
    for stage in range(DEG):
        outer = from_next_chip(edge)
        other_inner = from_other_core(inner)
        other_edge = from_other_core(edge)
        edge_partial = plane_part(edge, edge_level, weights)
        inner_partial = plane_part(inner, inner_level, weights)
        inner_next = layer_part(layers, inner_partial, inner, other_inner, other_edge, inner_before)
        last = inner_next if stage == DEG - 1 else None
        edge_next = layer_part(layers, edge_partial, edge, outer, other_inner, edge_before, last)
        edge_before, edge = edge, edge_next
        inner_before, inner = inner, inner_next
    return edge


def join_kernel(bricks_y, *refs):
    parts = owned * bricks_y
    received_refs, (cells_ref, gram_ref, block_ref) = refs[:parts], refs[parts:]
    mid, y = lax.axis_index("mid"), lax.axis_index("gy")
    columns, plane = block_ref.shape
    share = columns // parts
    layers = cells_ref.shape[0] // plane
    total = None
    for layer in range(layers):
        for step, received_ref in zip(offsets(bricks_y), received_refs):
            from_mid, from_y = behind(mid, y, step, bricks_y)
            first = pl.multiple_of((from_mid * bricks_y + from_y) * share, share)
            own = received_ref[layer * share : (layer + 1) * share, :]
            block_ref[pl.ds(first, share), :] = own.astype(jnp.float32)
        block = block_ref[...]
        cells_ref[layer * plane : (layer + 1) * plane, :] = block.T.astype(jnp.bfloat16)
        narrow = block.astype(jnp.bfloat16)
        part = lax.dot_general(
            narrow, narrow, (((1,), (1,)), ((), ())), preferred_element_type=jnp.float32
        )
        total = part if total is None else total + part
    half = columns // 2
    packed = jnp.concatenate([total[:half], total[half:, half:]], axis=1)
    piece = gram_ref.shape[1]
    for device in range(gram_ref.shape[0]):
        gram_ref[device] = packed[device * piece : (device + 1) * piece]


def join_columns(received, layers, bricks_y):
    rows, plane = received[0].shape
    columns = rows // layers * owned * bricks_y
    half = columns // 2
    shares = math.gcd(lax.axis_size(axes), half)
    return pl.pallas_call(
        functools.partial(join_kernel, bricks_y),
        out_shape=(
            jax.ShapeDtypeStruct((layers * plane, columns), jnp.bfloat16),
            jax.ShapeDtypeStruct((shares, half // shares, 3 * half), jnp.float32),
        ),
        scratch_shapes=[pltpu.VMEM((columns, plane), jnp.float32)],
        compiler_params=pltpu.CompilerParams(vmem_limit_bytes=vmem_limit),
    )(*received)


lanes = 128
panel_rows = 8
block_rows = 64


def row_splat(values, row):
    return jnp.broadcast_to(values[row : row + 1, :], values.shape)


def lane_splat(values, lane):
    return jnp.broadcast_to(values[:, lane : lane + 1], (panel_rows, lanes))


def panel_inverse(columns):
    row = lax.broadcasted_iota(jnp.int32, (panel_rows, lanes), 0)
    columns = list(columns)
    full = [jnp.where(row == k, 1.0, 0.0).astype(jnp.float32) for k in range(panel_rows)]
    forward = list(full)
    scales = jnp.zeros((panel_rows, lanes), jnp.float32)
    for step in range(panel_rows):
        scale = 1.0 / row_splat(columns[step], step)
        scales = jnp.where(row == step, scale, scales)
        others = jnp.where(row == step, 0.0, columns[step])
        for k in range(step + 1, panel_rows):
            columns[k] = columns[k] - others * (row_splat(columns[k], step) * scale)
        for k in range(step):
            forward[k] = jnp.where(row == step, full[k], forward[k])
            full[k] = full[k] - others * (row_splat(full[k], step) * scale)
        full[step] = full[step] - others * scale
    root = jnp.sqrt(scales)
    full = [column * scales for column in full]
    forward = [column * root for column in forward]
    return full, forward


def combine(columns, rows):
    parts = []
    for left in range(0, rows.shape[1], lanes):
        piece = rows[:, left : left + lanes]
        terms = [column * row_splat(piece, k) for k, column in enumerate(columns)]
        while len(terms) > 1:
            terms = [a + b for a, b in zip(terms[::2], terms[1::2])]
        parts.append(terms[0])
    return jnp.concatenate(parts, axis=1)


def factor_kernel(scale, gram_ref, rows_ref, rotated_ref, upper_ref, packed_ref, factor_ref, inverse_ref):
    shares, piece, width = gram_ref.shape
    half = shares * piece
    order = 2 * half
    for share in range(shares):
        packed_ref[share * piece : (share + 1) * piece, :] = gram_ref[share]
    factor_ref[...] = jnp.zeros((order, order), jnp.float32)
    inverse_ref[...] = jnp.zeros((order, order), jnp.float32)
    for start in range(0, order, block_rows):
        left = start // lanes * lanes
        right = left + lanes
        local = start - left
        row = lax.broadcasted_iota(jnp.int32, (block_rows, right), 0)
        col = lax.broadcasted_iota(jnp.int32, (block_rows, right), 1)
        unit = jnp.where(col == row + start, 1.0, 0.0).astype(jnp.float32)
        at, side = (start, 0) if start < half else (start - half, order)
        own = packed_ref[at : at + block_rows, side : side + order - left]
        block = jnp.concatenate([own, unit], axis=1)
        if start > 0:
            done = jnp.concatenate(
                [factor_ref[:start, left:order], inverse_ref[:start, :right]], axis=1
            )
            update = lax.dot_general(
                factor_ref[:start, left : left + lanes],
                done,
                (((0,), (0,)), ((), ())),
                precision=lax.Precision.HIGHEST,
                preferred_element_type=jnp.float32,
            )
            block = block - update[local : local + block_rows]
        groups = [
            block[g : g + panel_rows] for g in range(0, block_rows, panel_rows)
        ]
        for index in range(len(groups)):
            lane = local + index * panel_rows
            rows = groups[index]
            full, forward = panel_inverse([lane_splat(rows, lane + k) for k in range(panel_rows)])
            step_rows = combine(full, rows)
            for other in range(index + 1, len(groups)):
                target = groups[other]
                columns = [lane_splat(target, lane + k) for k in range(panel_rows)]
                groups[other] = target - combine(columns, step_rows)
            finished = combine(forward, rows)
            at = start + index * panel_rows
            factor_ref[at : at + panel_rows, left:order] = finished[:, : order - left]
            inverse_ref[at : at + panel_rows, :right] = finished[:, order - left :]
    row = lax.broadcasted_iota(jnp.int32, (order, order), 0)
    col = lax.broadcasted_iota(jnp.int32, (order, order), 1)
    upper_ref[...] = jnp.where(col >= row, factor_ref[...] * (1.0 / scale), 0.0)
    inverse = jnp.where(col <= row, inverse_ref[...] * scale, 0.0)
    high = inverse.astype(jnp.bfloat16)
    rest = inverse - high.astype(jnp.float32)
    middle = rest.astype(jnp.bfloat16)
    low = (rest - middle.astype(jnp.float32)).astype(jnp.bfloat16)
    count = rows_ref.shape[0]
    chunk = math.gcd(count, 512)
    for at in range(0, count, chunk):
        piece = rows_ref[at : at + chunk, :]
        total = jnp.zeros((chunk, order), jnp.float32)
        for part in (low, middle, high):
            total = total + lax.dot_general(
                piece, part, (((1,), (1,)), ((), ())), preferred_element_type=jnp.float32
            )
        rotated_ref[at : at + chunk, :] = total.astype(jnp.bfloat16)


def factor_and_rotate(gram_matrix, rows, total_cells):
    order = rows.shape[1]
    count = rows.shape[0]
    return pl.pallas_call(
        functools.partial(factor_kernel, math.sqrt(total_cells)),
        out_shape=(
            jax.ShapeDtypeStruct((count, order), jnp.bfloat16),
            jax.ShapeDtypeStruct((order, order), jnp.float32),
        ),
        scratch_shapes=[
            pltpu.VMEM((order // 2, order // 2 * 3), jnp.float32),
            pltpu.VMEM((order, order), jnp.float32),
            pltpu.VMEM((order, order), jnp.float32),
        ],
        compiler_params=pltpu.CompilerParams(vmem_limit_bytes=vmem_limit),
    )(gram_matrix, rows)


def sum_over_devices(values):
    if lax.axis_size(axes) != values.shape[0]:
        return lax.psum(values, axes)
    total = jnp.sum(lax.all_to_all(values, axes, 0, 0), axis=0)
    return lax.all_to_all(jnp.broadcast_to(total[None], values.shape), axes, 0, 0)


def shards(trial_orbitals, potential):
    layers, extent_y, extent_z, columns = trial_orbitals.shape
    bricks_y = lax.axis_size("gy")
    total_cells = lax.axis_size(axes) * layers * extent_y * extent_z
    weights = jnp.asarray(plane_weights(extent_y, extent_z))

    cells = trial_orbitals.reshape(layers * extent_y * extent_z, columns)
    sent = split_columns(cells, potential, bricks_y)
    placed = place(exchange(sent, bricks_y), layers, bricks_y)
    sent = chebyshev(*placed, weights)
    rows, local_gram = join_columns(exchange(sent, bricks_y), layers, bricks_y)
    gram_matrix = sum_over_devices(local_gram)
    rotated, upper_factor = factor_and_rotate(gram_matrix, rows, total_cells)
    return (rotated.reshape(trial_orbitals.shape), upper_factor)


def solution(mesh):
    bricks_x, bricks_y = mesh.devices.shape
    cut = Mesh(mesh.devices.reshape(bricks_x // 4, owned, 2, bricks_y), axes)
    cells = P(("far", "mid", "core"), "gy")
    return jax.shard_map(
        shards,
        mesh=cut,
        in_specs=(cells, cells),
        out_specs=(cells, P()),
        check_vma=False,
    )
```

```python
import functools
import math

import jax
import jax.numpy as jnp
import ml_dtypes
import numpy as np
from jax import lax
from jax.experimental import pallas as pl
from jax.experimental.pallas import tpu as pltpu
from jax.sharding import Mesh, PartitionSpec as P

DEG = 3


STENCIL_WEIGHTS = (
    -5369.0 / 1800.0,
    12.0 / 7.0,
    -15.0 / 56.0,
    10.0 / 189.0,
    -1.0 / 112.0,
    2.0 / 1925.0,
    -1.0 / 16632.0,
)
stencil_reach = 6
filter_center = 11.5
filter_half = 8.5
axes = ("far", "mid", "core", "gy")
owned = 2
group = 16
vmem_limit = 48 * 1024 * 1024

center_shift = -1.5 * STENCIL_WEIGHTS[0] - filter_center
side_weights = tuple(-0.5 * weight / filter_half for weight in STENCIL_WEIGHTS)


def bfloat16_parts(values):
    parts = []
    rest = np.asarray(values, np.float32)
    for _ in range(3):
        part = rest.astype(ml_dtypes.bfloat16)
        parts.append(part)
        rest = rest - part.astype(np.float32)
    return np.stack(parts)


def plane_weights(extent_y, extent_z):
    def band(extent, shift):
        matrix = np.zeros((extent, extent), np.float64)
        for source in range(extent):
            for target in range(extent):
                distance = abs(target - (source + shift))
                if 1 <= distance <= stencil_reach:
                    matrix[source, target] = side_weights[distance]
        return matrix

    eye_y, eye_z = np.eye(extent_y), np.eye(extent_z)
    own = np.kron(band(extent_y, 0), eye_z) + np.kron(eye_y, band(extent_z, 0))
    before = np.kron(band(extent_y, -extent_y), eye_z)
    after = np.kron(band(extent_y, extent_y), eye_z)
    return np.stack([bfloat16_parts(part) for part in (own, before, after)])


def level_rows(potential, rows):
    rest = (potential + center_shift) * (1.0 / filter_half)
    parts = []
    for _ in range(3):
        part = rest.astype(jnp.bfloat16).astype(jnp.float32)
        parts.append(part)
        rest = rest - part
    unused = jnp.zeros((rows - 3 * rest.shape[0], rest.shape[1]), jnp.float32)
    return jnp.concatenate(parts + [unused], axis=0).astype(jnp.bfloat16)


def level_room(layers):
    return -(-3 * layers // 16) * 16


def offsets(bricks_y):
    return [(i, j) for i in range(owned) for j in range(bricks_y)]


def ahead(mid, y, step, bricks_y):
    return lax.rem(mid + step[0], owned), lax.rem(y + step[1], bricks_y)


def behind(mid, y, step, bricks_y):
    return lax.rem(mid + step[0], owned), lax.rem(y - step[1] + bricks_y, bricks_y)


def exchange(messages, bricks_y):
    result = [messages[0]]
    for step, message in list(zip(offsets(bricks_y), messages))[1:]:
        perm = []
        for mid in range(owned):
            for y in range(bricks_y):
                target = (mid + step[0]) % owned * bricks_y + (y + step[1]) % bricks_y
                perm.append((mid * bricks_y + y, target))
        result.append(lax.ppermute(message, ("mid", "gy"), perm))
    return result


def split_kernel(bricks_y, cells_ref, potential_ref, *refs):
    sent_refs, block_ref = refs[:-1], refs[-1]
    mid, y = lax.axis_index("mid"), lax.axis_index("gy")
    columns, plane = block_ref.shape
    share = columns // len(sent_refs)
    layers = cells_ref.shape[0] // plane
    potential = jnp.concatenate(
        [potential_ref[:, at, :] for at in range(potential_ref.shape[1])], axis=1
    )
    extra = level_rows(potential, sent_refs[0].shape[0] - layers * share)
    for sent_ref in sent_refs:
        sent_ref[layers * share :, :] = extra
    for layer in range(layers):
        block = cells_ref[layer * plane : (layer + 1) * plane, :].astype(jnp.float32)
        block_ref[...] = block.T
        for step, sent_ref in zip(offsets(bricks_y), sent_refs):
            to_mid, to_y = ahead(mid, y, step, bricks_y)
            first = pl.multiple_of((to_mid * bricks_y + to_y) * share, share)
            own = block_ref[pl.ds(first, share), :]
            sent_ref[layer * share : (layer + 1) * share, :] = own.astype(jnp.bfloat16)


def split_columns(cells, potential, bricks_y):
    count, columns = cells.shape
    layers = potential.shape[0]
    plane = count // layers
    parts = owned * bricks_y
    message = jax.ShapeDtypeStruct(
        (layers * (columns // parts) + level_room(layers), plane), jnp.bfloat16
    )
    return pl.pallas_call(
        functools.partial(split_kernel, bricks_y),
        out_shape=[message] * parts,
        scratch_shapes=[pltpu.VMEM((columns, plane), jnp.float32)],
        compiler_params=pltpu.CompilerParams(vmem_limit_bytes=vmem_limit),
    )(cells, potential)


def place_kernel(bricks_y, *refs):
    parts = owned * bricks_y
    received_refs, results = refs[:parts], refs[parts:]
    edge_ref, inner_ref, edge_level_ref, inner_level_ref, own_ref, level_ref = results
    mid, y, core = lax.axis_index("mid"), lax.axis_index("gy"), lax.axis_index("core")
    rows = own_ref.shape[2]
    layers = level_ref.shape[2]
    for step, received_ref in zip(offsets(bricks_y), received_refs):
        at, b = behind(mid, y, step, bricks_y)
        own_ref[at, b] = received_ref[:rows]
        extra = received_ref[rows:].astype(jnp.float32)
        level = extra[:layers] + extra[layers : 2 * layers] + extra[2 * layers : 3 * layers]
        level_ref[at, b] = level
    edge_ref[...] = own_ref[core]
    inner_ref[...] = own_ref[1 - core]
    edge_level_ref[...] = level_ref[core]
    inner_level_ref[...] = level_ref[1 - core]


def place(received, layers, bricks_y):
    plane = received[0].shape[1]
    rows = received[0].shape[0] - level_room(layers)
    field = (bricks_y, rows, plane)
    level = (bricks_y, layers, plane)
    return pl.pallas_call(
        functools.partial(place_kernel, bricks_y),
        out_shape=[jax.ShapeDtypeStruct(field, jnp.bfloat16)] * 2
        + [jax.ShapeDtypeStruct(level, jnp.float32)] * 2,
        scratch_shapes=[
            pltpu.VMEM((owned,) + field, jnp.bfloat16),
            pltpu.VMEM((owned,) + level, jnp.float32),
        ],
        compiler_params=pltpu.CompilerParams(vmem_limit_bytes=vmem_limit),
    )(*received)


def plane_kernel(own_ref, level_ref, weights_ref, partial_ref):
    bricks_y, rows, plane = own_ref.shape
    layers = level_ref.shape[1]
    share = rows // layers
    for b in range(bricks_y):
        fields, weights = [], []
        for kind, other in ((0, b), (1, b - 1), (2, b + 1)):
            if 0 <= other < bricks_y:
                for part in range(weights_ref.shape[1]):
                    fields.append(own_ref[other])
                    weights.append(weights_ref[kind, part])
        sides = jnp.dot(
            jnp.concatenate(fields, axis=1),
            jnp.concatenate(weights, axis=0),
            preferred_element_type=jnp.float32,
        )
        for layer in range(layers):
            here = slice(layer * share, (layer + 1) * share)
            level = jnp.broadcast_to(level_ref[b, layer : layer + 1, :], (share, plane))
            partial_ref[b, here] = sides[here] + level * own_ref[b, here].astype(jnp.float32)


def plane_part(own, level, weights):
    bricks_y, rows, plane = own.shape
    flops = 2 * bricks_y * bricks_y * 3 * rows * plane * plane
    return pl.pallas_call(
        plane_kernel,
        out_shape=jax.ShapeDtypeStruct(own.shape, jnp.float32),
        cost_estimate=pl.CostEstimate(flops=flops, bytes_accessed=own.size * 6, transcendentals=0),
        compiler_params=pltpu.CompilerParams(vmem_limit_bytes=vmem_limit),
    )(own, level, weights)


def layer_kernel(first, layers, pack, partial_ref, own_ref, outer_ref, other_ref, *refs):
    refs = list(refs)
    before_ref = None if first else refs.pop(0)
    inner_ref = refs.pop(0) if pack else None
    next_ref = refs.pop()
    core, mid, y = lax.axis_index("core"), lax.axis_index("mid"), lax.axis_index("gy")
    bricks_y, rows, plane = own_ref.shape
    share = rows // layers
    width = min(plane, 128)

    def step(low_ref, high_ref):
        for b in range(bricks_y):
            for column in range(0, share, group):
                for left in range(0, plane, width):
                    lane = slice(left, left + width)
                    places = [
                        slice(layer * share + column, layer * share + column + group)
                        for layer in range(layers)
                    ]
                    window = [
                        ref[b, here, lane].astype(jnp.float32)
                        for ref in (low_ref, own_ref, high_ref)
                        for here in places
                    ]
                    for layer, here in enumerate(places):
                        value = partial_ref[b, here, lane]
                        for distance in range(1, stencil_reach + 1):
                            pair = window[layers + layer - distance] + window[layers + layer + distance]
                            value = value + side_weights[distance] * pair
                        if before_ref is not None:
                            value = 2.0 * value - before_ref[b, here, lane].astype(jnp.float32)
                        next_ref[b, here, lane] = value.astype(jnp.bfloat16)

    @pl.when(core == 0)
    def _():
        step(outer_ref, other_ref)

    @pl.when(core != 0)
    def _():
        step(other_ref, outer_ref)

    if pack:
        for offset, sent_ref in zip(offsets(bricks_y), refs):
            to_mid, to_y = ahead(mid, y, offset, bricks_y)

            @pl.when(to_mid == core)
            def _():
                sent_ref[...] = next_ref[to_y]

            @pl.when(to_mid != core)
            def _():
                sent_ref[...] = inner_ref[to_y]


def layer_part(layers, partial, own, outer, other, before, inner=None):
    bricks_y, rows, plane = own.shape
    pack = inner is not None
    operands = [partial, own, outer, other]
    operands += [] if before is None else [before]
    operands += [inner] if pack else []
    one = jax.ShapeDtypeStruct((rows, plane), jnp.bfloat16)
    return pl.pallas_call(
        functools.partial(layer_kernel, before is None, layers, pack),
        out_shape=[one] * (owned * bricks_y) if pack else jax.ShapeDtypeStruct(own.shape, jnp.bfloat16),
        scratch_shapes=[pltpu.VMEM(own.shape, jnp.bfloat16)] if pack else [],
        cost_estimate=pl.CostEstimate(
            flops=24 * own.size, bytes_accessed=own.size * 14, transcendentals=0
        ),
        compiler_params=pltpu.CompilerParams(vmem_limit_bytes=vmem_limit),
    )(*operands)


def from_other_core(own):
    return lax.ppermute(own, "core", [(0, 1), (1, 0)])


def from_next_chip(edge):
    count = lax.axis_size(("far", "core"))
    pairs = [(at, at + 1) for at in range(1, count - 1, 2)]
    return lax.ppermute(edge, ("far", "core"), pairs + [(b, a) for a, b in pairs])


def chebyshev(edge, inner, edge_level, inner_level, weights):
    layers = edge_level.shape[1]
    edge_before = inner_before = None
    for stage in range(DEG):
        outer = from_next_chip(edge)
        other_inner = from_other_core(inner)
        other_edge = from_other_core(edge)
        edge_partial = plane_part(edge, edge_level, weights)
        inner_partial = plane_part(inner, inner_level, weights)
        inner_next = layer_part(layers, inner_partial, inner, other_inner, other_edge, inner_before)
        last = inner_next if stage == DEG - 1 else None
        edge_next = layer_part(layers, edge_partial, edge, outer, other_inner, edge_before, last)
        edge_before, edge = edge, edge_next
        inner_before, inner = inner, inner_next
    return edge


def join_kernel(bricks_y, *refs):
    parts = owned * bricks_y
    received_refs, (cells_ref, gram_ref, block_ref) = refs[:parts], refs[parts:]
    mid, y = lax.axis_index("mid"), lax.axis_index("gy")
    columns, plane = block_ref.shape
    share = columns // parts
    layers = cells_ref.shape[0] // plane
    total = None
    for layer in range(layers):
        for step, received_ref in zip(offsets(bricks_y), received_refs):
            from_mid, from_y = behind(mid, y, step, bricks_y)
            first = pl.multiple_of((from_mid * bricks_y + from_y) * share, share)
            own = received_ref[layer * share : (layer + 1) * share, :]
            block_ref[pl.ds(first, share), :] = own.astype(jnp.float32)
        block = block_ref[...]
        cells_ref[layer * plane : (layer + 1) * plane, :] = block.T.astype(jnp.bfloat16)
        narrow = block.astype(jnp.bfloat16)
        part = lax.dot_general(
            narrow, narrow, (((1,), (1,)), ((), ())), preferred_element_type=jnp.float32
        )
        total = part if total is None else total + part
    half = columns // 2
    packed = jnp.concatenate([total[:half], total[half:, half:]], axis=1)
    piece = gram_ref.shape[1]
    for device in range(gram_ref.shape[0]):
        gram_ref[device] = packed[device * piece : (device + 1) * piece]


def join_columns(received, layers, bricks_y):
    rows, plane = received[0].shape
    columns = rows // layers * owned * bricks_y
    half = columns // 2
    shares = math.gcd(lax.axis_size(axes), half)
    return pl.pallas_call(
        functools.partial(join_kernel, bricks_y),
        out_shape=(
            jax.ShapeDtypeStruct((layers * plane, columns), jnp.bfloat16),
            jax.ShapeDtypeStruct((shares, half // shares, 3 * half), jnp.float32),
        ),
        scratch_shapes=[pltpu.VMEM((columns, plane), jnp.float32)],
        compiler_params=pltpu.CompilerParams(vmem_limit_bytes=vmem_limit),
    )(*received)


lanes = 128
panel_rows = 8
block_rows = 64


def row_splat(values, row):
    return jnp.broadcast_to(values[row : row + 1, :], values.shape)


def lane_splat(values, lane):
    return jnp.broadcast_to(values[:, lane : lane + 1], (panel_rows, lanes))


def panel_inverse(columns):
    size = range(panel_rows)
    entry = {(i, k): row_splat(columns[k], i) for k in size for i in range(k + 1)}
    scale, multiplier, unit = {}, {}, {}
    for step in size:
        scale[step] = 1.0 / entry[step, step]
        for k in range(step + 1, panel_rows):
            multiplier[step, k] = entry[step, k] * scale[step]
            for i in range(step + 1, k + 1):
                entry[i, k] = entry[i, k] - entry[step, k] * multiplier[step, i]
        for k in range(step):
            total = multiplier[k, step]
            for between in range(k + 1, step):
                total = total + multiplier[between, step] * unit[between, k]
            unit[step, k] = -total
    row = lax.broadcasted_iota(jnp.int32, (panel_rows, lanes), 0)
    columns = list(columns)
    full = [jnp.where(row == k, 1.0, 0.0).astype(jnp.float32) for k in size]
    forward = list(full)
    scales = scale[0]
    for step in size:
        others = jnp.where(row == step, 0.0, columns[step])
        scales = jnp.where(row == step, scale[step], scales)
        for k in range(step + 1, panel_rows):
            columns[k] = columns[k] - others * multiplier[step, k]
        for k in range(step):
            forward[k] = jnp.where(row == step, unit[step, k], forward[k])
            full[k] = full[k] - others * (unit[step, k] * scale[step])
        full[step] = full[step] - others * scale[step]
    root = jnp.sqrt(scales)
    full = [column * scales for column in full]
    forward = [column * root for column in forward]
    return full, forward


def combine(columns, rows):
    parts = []
    for left in range(0, rows.shape[1], lanes):
        piece = rows[:, left : left + lanes]
        terms = [column * row_splat(piece, k) for k, column in enumerate(columns)]
        while len(terms) > 1:
            terms = [a + b for a, b in zip(terms[::2], terms[1::2])]
        parts.append(terms[0])
    return jnp.concatenate(parts, axis=1)


def factor_kernel(scale, gram_ref, rows_ref, rotated_ref, upper_ref, packed_ref, factor_ref, inverse_ref):
    shares, piece, width = gram_ref.shape
    half = shares * piece
    order = 2 * half
    for share in range(shares):
        packed_ref[share * piece : (share + 1) * piece, :] = gram_ref[share]
    factor_ref[...] = jnp.zeros((order, order), jnp.float32)
    inverse_ref[...] = jnp.zeros((order, order), jnp.float32)
    for start in range(0, order, block_rows):
        left = start // lanes * lanes
        right = left + lanes
        local = start - left
        row = lax.broadcasted_iota(jnp.int32, (block_rows, right), 0)
        col = lax.broadcasted_iota(jnp.int32, (block_rows, right), 1)
        unit = jnp.where(col == row + start, 1.0, 0.0).astype(jnp.float32)
        at, side = (start, 0) if start < half else (start - half, order)
        own = packed_ref[at : at + block_rows, side : side + order - left]
        block = jnp.concatenate([own, unit], axis=1)
        if start > 0:
            done = jnp.concatenate(
                [factor_ref[:start, left:order], inverse_ref[:start, :right]], axis=1
            )
            update = lax.dot_general(
                factor_ref[:start, left : left + lanes],
                done,
                (((0,), (0,)), ((), ())),
                precision=lax.Precision.HIGHEST,
                preferred_element_type=jnp.float32,
            )
            block = block - update[local : local + block_rows]
        groups = [
            block[g : g + panel_rows] for g in range(0, block_rows, panel_rows)
        ]
        for index in range(len(groups)):
            lane = local + index * panel_rows
            rows = groups[index]
            full, forward = panel_inverse([lane_splat(rows, lane + k) for k in range(panel_rows)])
            step_rows = combine(full, rows)
            for other in range(index + 1, len(groups)):
                target = groups[other]
                columns = [lane_splat(target, lane + k) for k in range(panel_rows)]
                groups[other] = target - combine(columns, step_rows)
            finished = combine(forward, rows)
            at = start + index * panel_rows
            factor_ref[at : at + panel_rows, left:order] = finished[:, : order - left]
            inverse_ref[at : at + panel_rows, :right] = finished[:, order - left :]
    row = lax.broadcasted_iota(jnp.int32, (order, order), 0)
    col = lax.broadcasted_iota(jnp.int32, (order, order), 1)
    upper_ref[...] = jnp.where(col >= row, factor_ref[...] * (1.0 / scale), 0.0)
    inverse = jnp.where(col <= row, inverse_ref[...] * scale, 0.0)
    high = inverse.astype(jnp.bfloat16)
    rest = inverse - high.astype(jnp.float32)
    middle = rest.astype(jnp.bfloat16)
    low = (rest - middle.astype(jnp.float32)).astype(jnp.bfloat16)
    count = rows_ref.shape[0]
    chunk = math.gcd(count, 512)
    for at in range(0, count, chunk):
        piece = rows_ref[at : at + chunk, :]
        total = jnp.zeros((chunk, order), jnp.float32)
        for part in (low, middle, high):
            total = total + lax.dot_general(
                piece, part, (((1,), (1,)), ((), ())), preferred_element_type=jnp.float32
            )
        rotated_ref[at : at + chunk, :] = total.astype(jnp.bfloat16)


def factor_and_rotate(gram_matrix, rows, total_cells):
    order = rows.shape[1]
    count = rows.shape[0]
    return pl.pallas_call(
        functools.partial(factor_kernel, math.sqrt(total_cells)),
        out_shape=(
            jax.ShapeDtypeStruct((count, order), jnp.bfloat16),
            jax.ShapeDtypeStruct((order, order), jnp.float32),
        ),
        scratch_shapes=[
            pltpu.VMEM((order // 2, order // 2 * 3), jnp.float32),
            pltpu.VMEM((order, order), jnp.float32),
            pltpu.VMEM((order, order), jnp.float32),
        ],
        compiler_params=pltpu.CompilerParams(vmem_limit_bytes=vmem_limit),
    )(gram_matrix, rows)


def sum_over_devices(values):
    if lax.axis_size(axes) != values.shape[0]:
        return lax.psum(values, axes)
    total = jnp.sum(lax.all_to_all(values, axes, 0, 0), axis=0)
    return lax.all_to_all(jnp.broadcast_to(total[None], values.shape), axes, 0, 0)


def shards(trial_orbitals, potential):
    layers, extent_y, extent_z, columns = trial_orbitals.shape
    bricks_y = lax.axis_size("gy")
    total_cells = lax.axis_size(axes) * layers * extent_y * extent_z
    weights = jnp.asarray(plane_weights(extent_y, extent_z))

    cells = trial_orbitals.reshape(layers * extent_y * extent_z, columns)
    sent = split_columns(cells, potential, bricks_y)
    placed = place(exchange(sent, bricks_y), layers, bricks_y)
    sent = chebyshev(*placed, weights)
    rows, local_gram = join_columns(exchange(sent, bricks_y), layers, bricks_y)
    gram_matrix = sum_over_devices(local_gram)
    rotated, upper_factor = factor_and_rotate(gram_matrix, rows, total_cells)
    return (rotated.reshape(trial_orbitals.shape), upper_factor)


def solution(mesh):
    bricks_x, bricks_y = mesh.devices.shape
    cut = Mesh(mesh.devices.reshape(bricks_x // 4, owned, 2, bricks_y), axes)
    cells = P(("far", "mid", "core"), "gy")
    return jax.shard_map(
        shards,
        mesh=cut,
        in_specs=(cells, cells),
        out_specs=(cells, P()),
        check_vma=False,
    )
```

```python
import functools
import math

import jax
import jax.numpy as jnp
import ml_dtypes
import numpy as np
from jax import lax
from jax.experimental import pallas as pl
from jax.experimental.pallas import tpu as pltpu
from jax.sharding import Mesh, PartitionSpec as P

DEG = 3


STENCIL_WEIGHTS = (
    -5369.0 / 1800.0,
    12.0 / 7.0,
    -15.0 / 56.0,
    10.0 / 189.0,
    -1.0 / 112.0,
    2.0 / 1925.0,
    -1.0 / 16632.0,
)
stencil_reach = 6
filter_center = 11.5
filter_half = 8.5
axes = ("far", "mid", "core", "gy")
owned = 2
group = 16
vmem_limit = 48 * 1024 * 1024

center_shift = -1.5 * STENCIL_WEIGHTS[0] - filter_center
side_weights = tuple(-0.5 * weight / filter_half for weight in STENCIL_WEIGHTS)


def bfloat16_parts(values):
    parts = []
    rest = np.asarray(values, np.float32)
    for _ in range(3):
        part = rest.astype(ml_dtypes.bfloat16)
        parts.append(part)
        rest = rest - part.astype(np.float32)
    return np.stack(parts)


def plane_weights(extent_y, extent_z):
    def band(extent, shift):
        matrix = np.zeros((extent, extent), np.float64)
        for source in range(extent):
            for target in range(extent):
                distance = abs(target - (source + shift))
                if 1 <= distance <= stencil_reach:
                    matrix[source, target] = side_weights[distance]
        return matrix

    eye_y, eye_z = np.eye(extent_y), np.eye(extent_z)
    own = np.kron(band(extent_y, 0), eye_z) + np.kron(eye_y, band(extent_z, 0))
    before = np.kron(band(extent_y, -extent_y), eye_z)
    after = np.kron(band(extent_y, extent_y), eye_z)
    return np.stack([bfloat16_parts(part) for part in (own, before, after)])


def level_rows(potential, rows):
    rest = (potential + center_shift) * (1.0 / filter_half)
    parts = []
    for _ in range(3):
        part = rest.astype(jnp.bfloat16).astype(jnp.float32)
        parts.append(part)
        rest = rest - part
    unused = jnp.zeros((rows - 3 * rest.shape[0], rest.shape[1]), jnp.float32)
    return jnp.concatenate(parts + [unused], axis=0).astype(jnp.bfloat16)


def level_room(layers):
    return -(-3 * layers // 16) * 16


def offsets(bricks_y):
    return [(i, j) for i in range(owned) for j in range(bricks_y)]


def ahead(mid, y, step, bricks_y):
    return lax.rem(mid + step[0], owned), lax.rem(y + step[1], bricks_y)


def behind(mid, y, step, bricks_y):
    return lax.rem(mid + step[0], owned), lax.rem(y - step[1] + bricks_y, bricks_y)


def exchange(messages, bricks_y):
    result = [messages[0]]
    for step, message in list(zip(offsets(bricks_y), messages))[1:]:
        perm = []
        for mid in range(owned):
            for y in range(bricks_y):
                target = (mid + step[0]) % owned * bricks_y + (y + step[1]) % bricks_y
                perm.append((mid * bricks_y + y, target))
        result.append(lax.ppermute(message, ("mid", "gy"), perm))
    return result


def split_kernel(bricks_y, cells_ref, potential_ref, *refs):
    sent_refs, block_ref = refs[:-1], refs[-1]
    mid, y = lax.axis_index("mid"), lax.axis_index("gy")
    columns, plane = block_ref.shape
    share = columns // len(sent_refs)
    layers = cells_ref.shape[0] // plane
    potential = jnp.concatenate(
        [potential_ref[:, at, :] for at in range(potential_ref.shape[1])], axis=1
    )
    extra = level_rows(potential, sent_refs[0].shape[0] - layers * share)
    for sent_ref in sent_refs:
        sent_ref[layers * share :, :] = extra
    for layer in range(layers):
        block = cells_ref[layer * plane : (layer + 1) * plane, :].astype(jnp.float32)
        block_ref[...] = block.T
        for step, sent_ref in zip(offsets(bricks_y), sent_refs):
            to_mid, to_y = ahead(mid, y, step, bricks_y)
            first = pl.multiple_of((to_mid * bricks_y + to_y) * share, share)
            own = block_ref[pl.ds(first, share), :]
            sent_ref[layer * share : (layer + 1) * share, :] = own.astype(jnp.bfloat16)


def split_columns(cells, potential, bricks_y):
    count, columns = cells.shape
    layers = potential.shape[0]
    plane = count // layers
    parts = owned * bricks_y
    message = jax.ShapeDtypeStruct(
        (layers * (columns // parts) + level_room(layers), plane), jnp.bfloat16
    )
    return pl.pallas_call(
        functools.partial(split_kernel, bricks_y),
        out_shape=[message] * parts,
        scratch_shapes=[pltpu.VMEM((columns, plane), jnp.float32)],
        compiler_params=pltpu.CompilerParams(vmem_limit_bytes=vmem_limit),
    )(cells, potential)


def place_kernel(bricks_y, *refs):
    parts = owned * bricks_y
    received_refs, results = refs[:parts], refs[parts:]
    edge_ref, inner_ref, edge_level_ref, inner_level_ref, own_ref, level_ref = results
    mid, y, core = lax.axis_index("mid"), lax.axis_index("gy"), lax.axis_index("core")
    rows = own_ref.shape[2]
    layers = level_ref.shape[2]
    for step, received_ref in zip(offsets(bricks_y), received_refs):
        at, b = behind(mid, y, step, bricks_y)
        own_ref[at, b] = received_ref[:rows]
        extra = received_ref[rows:].astype(jnp.float32)
        level = extra[:layers] + extra[layers : 2 * layers] + extra[2 * layers : 3 * layers]
        level_ref[at, b] = level
    edge_ref[...] = own_ref[core]
    inner_ref[...] = own_ref[1 - core]
    edge_level_ref[...] = level_ref[core]
    inner_level_ref[...] = level_ref[1 - core]


def place(received, layers, bricks_y):
    plane = received[0].shape[1]
    rows = received[0].shape[0] - level_room(layers)
    field = (bricks_y, rows, plane)
    level = (bricks_y, layers, plane)
    return pl.pallas_call(
        functools.partial(place_kernel, bricks_y),
        out_shape=[jax.ShapeDtypeStruct(field, jnp.bfloat16)] * 2
        + [jax.ShapeDtypeStruct(level, jnp.float32)] * 2,
        scratch_shapes=[
            pltpu.VMEM((owned,) + field, jnp.bfloat16),
            pltpu.VMEM((owned,) + level, jnp.float32),
        ],
        compiler_params=pltpu.CompilerParams(vmem_limit_bytes=vmem_limit),
    )(*received)


def plane_kernel(own_ref, level_ref, weights_ref, partial_ref):
    bricks_y, rows, plane = own_ref.shape
    layers = level_ref.shape[1]
    share = rows // layers
    for b in range(bricks_y):
        fields, weights = [], []
        for kind, other in ((0, b), (1, b - 1), (2, b + 1)):
            if 0 <= other < bricks_y:
                for part in range(weights_ref.shape[1]):
                    fields.append(own_ref[other])
                    weights.append(weights_ref[kind, part])
        sides = jnp.dot(
            jnp.concatenate(fields, axis=1),
            jnp.concatenate(weights, axis=0),
            preferred_element_type=jnp.float32,
        )
        for layer in range(layers):
            here = slice(layer * share, (layer + 1) * share)
            level = jnp.broadcast_to(level_ref[b, layer : layer + 1, :], (share, plane))
            partial_ref[b, here] = sides[here] + level * own_ref[b, here].astype(jnp.float32)


def plane_part(own, level, weights):
    bricks_y, rows, plane = own.shape
    flops = 2 * bricks_y * bricks_y * 3 * rows * plane * plane
    return pl.pallas_call(
        plane_kernel,
        out_shape=jax.ShapeDtypeStruct(own.shape, jnp.float32),
        cost_estimate=pl.CostEstimate(flops=flops, bytes_accessed=own.size * 6, transcendentals=0),
        compiler_params=pltpu.CompilerParams(vmem_limit_bytes=vmem_limit),
    )(own, level, weights)


def layer_kernel(first, layers, pack, partial_ref, own_ref, outer_ref, other_ref, *refs):
    refs = list(refs)
    before_ref = None if first else refs.pop(0)
    inner_ref = refs.pop(0) if pack else None
    next_ref = refs.pop()
    core, mid, y = lax.axis_index("core"), lax.axis_index("mid"), lax.axis_index("gy")
    bricks_y, rows, plane = own_ref.shape
    share = rows // layers
    width = min(plane, 128)

    def step(low_ref, high_ref):
        for b in range(bricks_y):
            for column in range(0, share, group):
                for left in range(0, plane, width):
                    lane = slice(left, left + width)
                    places = [
                        slice(layer * share + column, layer * share + column + group)
                        for layer in range(layers)
                    ]
                    window = [
                        ref[b, here, lane].astype(jnp.float32)
                        for ref in (low_ref, own_ref, high_ref)
                        for here in places
                    ]
                    for layer, here in enumerate(places):
                        value = partial_ref[b, here, lane]
                        for distance in range(1, stencil_reach + 1):
                            pair = window[layers + layer - distance] + window[layers + layer + distance]
                            value = value + side_weights[distance] * pair
                        if before_ref is not None:
                            value = 2.0 * value - before_ref[b, here, lane].astype(jnp.float32)
                        next_ref[b, here, lane] = value.astype(jnp.bfloat16)

    @pl.when(core == 0)
    def _():
        step(outer_ref, other_ref)

    @pl.when(core != 0)
    def _():
        step(other_ref, outer_ref)

    if pack:
        for offset, sent_ref in zip(offsets(bricks_y), refs):
            to_mid, to_y = ahead(mid, y, offset, bricks_y)

            @pl.when(to_mid == core)
            def _():
                sent_ref[...] = next_ref[to_y]

            @pl.when(to_mid != core)
            def _():
                sent_ref[...] = inner_ref[to_y]


def layer_part(layers, partial, own, outer, other, before, inner=None):
    bricks_y, rows, plane = own.shape
    pack = inner is not None
    operands = [partial, own, outer, other]
    operands += [] if before is None else [before]
    operands += [inner] if pack else []
    one = jax.ShapeDtypeStruct((rows, plane), jnp.bfloat16)
    return pl.pallas_call(
        functools.partial(layer_kernel, before is None, layers, pack),
        out_shape=[one] * (owned * bricks_y) if pack else jax.ShapeDtypeStruct(own.shape, jnp.bfloat16),
        scratch_shapes=[pltpu.VMEM(own.shape, jnp.bfloat16)] if pack else [],
        cost_estimate=pl.CostEstimate(
            flops=24 * own.size, bytes_accessed=own.size * 14, transcendentals=0
        ),
        compiler_params=pltpu.CompilerParams(vmem_limit_bytes=vmem_limit),
    )(*operands)


def from_other_core(own):
    return lax.ppermute(own, "core", [(0, 1), (1, 0)])


def from_next_chip(edge):
    count = lax.axis_size(("far", "core"))
    pairs = [(at, at + 1) for at in range(1, count - 1, 2)]
    return lax.ppermute(edge, ("far", "core"), pairs + [(b, a) for a, b in pairs])


def chebyshev(edge, inner, edge_level, inner_level, weights):
    layers = edge_level.shape[1]
    edge_before = inner_before = None
    for stage in range(DEG):
        outer = from_next_chip(edge)
        other_inner = from_other_core(inner)
        other_edge = from_other_core(edge)
        edge_partial = plane_part(edge, edge_level, weights)
        inner_partial = plane_part(inner, inner_level, weights)
        inner_next = layer_part(layers, inner_partial, inner, other_inner, other_edge, inner_before)
        last = inner_next if stage == DEG - 1 else None
        edge_next = layer_part(layers, edge_partial, edge, outer, other_inner, edge_before, last)
        edge_before, edge = edge, edge_next
        inner_before, inner = inner, inner_next
    return edge


def join_kernel(bricks_y, *refs):
    parts = owned * bricks_y
    received_refs, (cells_ref, gram_ref, block_ref) = refs[:parts], refs[parts:]
    mid, y = lax.axis_index("mid"), lax.axis_index("gy")
    columns, plane = block_ref.shape
    share = columns // parts
    layers = cells_ref.shape[0] // plane
    total = None
    for layer in range(layers):
        for step, received_ref in zip(offsets(bricks_y), received_refs):
            from_mid, from_y = behind(mid, y, step, bricks_y)
            first = pl.multiple_of((from_mid * bricks_y + from_y) * share, share)
            own = received_ref[layer * share : (layer + 1) * share, :]
            block_ref[pl.ds(first, share), :] = own.astype(jnp.float32)
        block = block_ref[...]
        cells_ref[layer * plane : (layer + 1) * plane, :] = block.T.astype(jnp.bfloat16)
        narrow = block.astype(jnp.bfloat16)
        part = lax.dot_general(
            narrow, narrow, (((1,), (1,)), ((), ())), preferred_element_type=jnp.float32
        )
        total = part if total is None else total + part
    half = columns // 2
    packed = jnp.concatenate([total[:half], total[half:, half:]], axis=1)
    piece = gram_ref.shape[1]
    for device in range(gram_ref.shape[0]):
        gram_ref[device] = packed[device * piece : (device + 1) * piece]


def join_columns(received, layers, bricks_y):
    rows, plane = received[0].shape
    columns = rows // layers * owned * bricks_y
    half = columns // 2
    shares = math.gcd(lax.axis_size(axes), half)
    return pl.pallas_call(
        functools.partial(join_kernel, bricks_y),
        out_shape=(
            jax.ShapeDtypeStruct((layers * plane, columns), jnp.bfloat16),
            jax.ShapeDtypeStruct((shares, half // shares, 3 * half), jnp.float32),
        ),
        scratch_shapes=[pltpu.VMEM((columns, plane), jnp.float32)],
        compiler_params=pltpu.CompilerParams(vmem_limit_bytes=vmem_limit),
    )(*received)


lanes = 128
panel_rows = 8
block_rows = 64


def row_splat(values, row):
    return jnp.broadcast_to(values[row : row + 1, :], values.shape)


def lane_splat(values, lane):
    return jnp.broadcast_to(values[:, lane : lane + 1], (panel_rows, lanes))


def panel_inverse(columns):
    row = lax.broadcasted_iota(jnp.int32, (panel_rows, lanes), 0)
    columns = list(columns)
    full = [jnp.where(row == k, 1.0, 0.0).astype(jnp.float32) for k in range(panel_rows)]
    forward = list(full)
    scales = jnp.zeros((panel_rows, lanes), jnp.float32)
    for step in range(panel_rows):
        scale = 1.0 / row_splat(columns[step], step)
        scales = jnp.where(row == step, scale, scales)
        others = jnp.where(row == step, 0.0, columns[step])
        for k in range(step + 1, panel_rows):
            columns[k] = columns[k] - others * (row_splat(columns[k], step) * scale)
        for k in range(step):
            forward[k] = jnp.where(row == step, full[k], forward[k])
            full[k] = full[k] - others * (row_splat(full[k], step) * scale)
        full[step] = full[step] - others * scale
    root = jnp.sqrt(scales)
    full = [column * scales for column in full]
    forward = [column * root for column in forward]
    return full, forward


def spread(rows):
    return [
        [row_splat(rows[:, left : left + lanes], k) for k in range(panel_rows)]
        for left in range(0, rows.shape[1], lanes)
    ]


def combine(columns, spread_rows):
    parts = []
    for rows in spread_rows:
        terms = [column * row for column, row in zip(columns, rows)]
        while len(terms) > 1:
            terms = [a + b for a, b in zip(terms[::2], terms[1::2])]
        parts.append(terms[0])
    return jnp.concatenate(parts, axis=1)


def factor_kernel(scale, gram_ref, rows_ref, rotated_ref, upper_ref, packed_ref, factor_ref, inverse_ref):
    shares, piece, width = gram_ref.shape
    half = shares * piece
    order = 2 * half
    for share in range(shares):
        packed_ref[share * piece : (share + 1) * piece, :] = gram_ref[share]
    factor_ref[...] = jnp.zeros((order, order), jnp.float32)
    inverse_ref[...] = jnp.zeros((order, order), jnp.float32)
    for start in range(0, order, block_rows):
        left = start // lanes * lanes
        right = left + lanes
        local = start - left
        row = lax.broadcasted_iota(jnp.int32, (block_rows, right), 0)
        col = lax.broadcasted_iota(jnp.int32, (block_rows, right), 1)
        unit = jnp.where(col == row + start, 1.0, 0.0).astype(jnp.float32)
        at, side = (start, 0) if start < half else (start - half, order)
        own = packed_ref[at : at + block_rows, side : side + order - left]
        block = jnp.concatenate([own, unit], axis=1)
        if start > 0:
            done = jnp.concatenate(
                [factor_ref[:start, left:order], inverse_ref[:start, :right]], axis=1
            )
            update = lax.dot_general(
                factor_ref[:start, left : left + lanes],
                done,
                (((0,), (0,)), ((), ())),
                precision=lax.Precision.HIGHEST,
                preferred_element_type=jnp.float32,
            )
            block = block - update[local : local + block_rows]
        groups = [
            block[g : g + panel_rows] for g in range(0, block_rows, panel_rows)
        ]
        for index in range(len(groups)):
            lane = local + index * panel_rows
            rows = groups[index]
            full, forward = panel_inverse([lane_splat(rows, lane + k) for k in range(panel_rows)])
            rows = spread(rows)
            step_rows = spread(combine(full, rows))
            for other in range(index + 1, len(groups)):
                target = groups[other]
                columns = [lane_splat(target, lane + k) for k in range(panel_rows)]
                groups[other] = target - combine(columns, step_rows)
            finished = combine(forward, rows)
            at = start + index * panel_rows
            factor_ref[at : at + panel_rows, left:order] = finished[:, : order - left]
            inverse_ref[at : at + panel_rows, :right] = finished[:, order - left :]
    row = lax.broadcasted_iota(jnp.int32, (order, order), 0)
    col = lax.broadcasted_iota(jnp.int32, (order, order), 1)
    upper_ref[...] = jnp.where(col >= row, factor_ref[...] * (1.0 / scale), 0.0)
    rest = jnp.where(col <= row, inverse_ref[...] * scale, 0.0).T
    parts = []
    for _ in range(3):
        parts.append(rest.astype(jnp.bfloat16))
        rest = rest - parts[-1].astype(jnp.float32)
    stacked = jnp.concatenate(parts, axis=0)
    count = rows_ref.shape[0]
    chunk = math.gcd(count, 512)
    for at in range(0, count, chunk):
        piece = rows_ref[at : at + chunk, :]
        total = jnp.dot(
            jnp.concatenate([piece] * len(parts), axis=1),
            stacked,
            preferred_element_type=jnp.float32,
        )
        rotated_ref[at : at + chunk, :] = total.astype(jnp.bfloat16)


def factor_and_rotate(gram_matrix, rows, total_cells):
    order = rows.shape[1]
    count = rows.shape[0]
    return pl.pallas_call(
        functools.partial(factor_kernel, math.sqrt(total_cells)),
        out_shape=(
            jax.ShapeDtypeStruct((count, order), jnp.bfloat16),
            jax.ShapeDtypeStruct((order, order), jnp.float32),
        ),
        scratch_shapes=[
            pltpu.VMEM((order // 2, order // 2 * 3), jnp.float32),
            pltpu.VMEM((order, order), jnp.float32),
            pltpu.VMEM((order, order), jnp.float32),
        ],
        compiler_params=pltpu.CompilerParams(vmem_limit_bytes=vmem_limit),
    )(gram_matrix, rows)


def sum_over_devices(values):
    if lax.axis_size(axes) != values.shape[0]:
        return lax.psum(values, axes)
    total = jnp.sum(lax.all_to_all(values, axes, 0, 0), axis=0)
    return lax.all_to_all(jnp.broadcast_to(total[None], values.shape), axes, 0, 0)


def shards(trial_orbitals, potential):
    layers, extent_y, extent_z, columns = trial_orbitals.shape
    bricks_y = lax.axis_size("gy")
    total_cells = lax.axis_size(axes) * layers * extent_y * extent_z
    weights = jnp.asarray(plane_weights(extent_y, extent_z))

    cells = trial_orbitals.reshape(layers * extent_y * extent_z, columns)
    sent = split_columns(cells, potential, bricks_y)
    placed = place(exchange(sent, bricks_y), layers, bricks_y)
    sent = chebyshev(*placed, weights)
    rows, local_gram = join_columns(exchange(sent, bricks_y), layers, bricks_y)
    gram_matrix = sum_over_devices(local_gram)
    rotated, upper_factor = factor_and_rotate(gram_matrix, rows, total_cells)
    return (rotated.reshape(trial_orbitals.shape), upper_factor)


def solution(mesh):
    bricks_x, bricks_y = mesh.devices.shape
    cut = Mesh(mesh.devices.reshape(bricks_x // 4, owned, 2, bricks_y), axes)
    cells = P(("far", "mid", "core"), "gy")
    return jax.shard_map(
        shards,
        mesh=cut,
        in_specs=(cells, cells),
        out_specs=(cells, P()),
        check_vma=False,
    )
```

```python
import functools
import math

import jax
import jax.numpy as jnp
import ml_dtypes
import numpy as np
from jax import lax
from jax.experimental import pallas as pl
from jax.experimental.pallas import tpu as pltpu
from jax.sharding import Mesh, PartitionSpec as P

DEG = 3


STENCIL_WEIGHTS = (
    -5369.0 / 1800.0,
    12.0 / 7.0,
    -15.0 / 56.0,
    10.0 / 189.0,
    -1.0 / 112.0,
    2.0 / 1925.0,
    -1.0 / 16632.0,
)
stencil_reach = 6
filter_center = 11.5
filter_half = 8.5
axes = ("far", "mid", "core", "gy")
owned = 2
group = 16
vmem_limit = 48 * 1024 * 1024

center_shift = -1.5 * STENCIL_WEIGHTS[0] - filter_center
side_weights = tuple(-0.5 * weight / filter_half for weight in STENCIL_WEIGHTS)


def bfloat16_parts(values):
    parts = []
    rest = np.asarray(values, np.float32)
    for _ in range(3):
        part = rest.astype(ml_dtypes.bfloat16)
        parts.append(part)
        rest = rest - part.astype(np.float32)
    return np.stack(parts)


def plane_weights(extent_y, extent_z):
    def band(extent, shift):
        matrix = np.zeros((extent, extent), np.float64)
        for source in range(extent):
            for target in range(extent):
                distance = abs(target - (source + shift))
                if 1 <= distance <= stencil_reach:
                    matrix[source, target] = side_weights[distance]
        return matrix

    eye_y, eye_z = np.eye(extent_y), np.eye(extent_z)
    own = np.kron(band(extent_y, 0), eye_z) + np.kron(eye_y, band(extent_z, 0))
    before = np.kron(band(extent_y, -extent_y), eye_z)
    after = np.kron(band(extent_y, extent_y), eye_z)
    return np.stack([bfloat16_parts(part) for part in (own, before, after)])


def level_rows(potential, rows):
    rest = (potential + center_shift) * (1.0 / filter_half)
    parts = []
    for _ in range(3):
        part = rest.astype(jnp.bfloat16).astype(jnp.float32)
        parts.append(part)
        rest = rest - part
    unused = jnp.zeros((rows - 3 * rest.shape[0], rest.shape[1]), jnp.float32)
    return jnp.concatenate(parts + [unused], axis=0).astype(jnp.bfloat16)


def level_room(layers):
    return -(-3 * layers // 16) * 16


def offsets(bricks_y):
    return [(i, j) for i in range(owned) for j in range(bricks_y)]


def ahead(mid, y, step, bricks_y):
    return lax.rem(mid + step[0], owned), lax.rem(y + step[1], bricks_y)


def behind(mid, y, step, bricks_y):
    return lax.rem(mid + step[0], owned), lax.rem(y - step[1] + bricks_y, bricks_y)


def exchange(messages, bricks_y):
    result = [messages[0]]
    for step, message in list(zip(offsets(bricks_y), messages))[1:]:
        perm = []
        for mid in range(owned):
            for y in range(bricks_y):
                target = (mid + step[0]) % owned * bricks_y + (y + step[1]) % bricks_y
                perm.append((mid * bricks_y + y, target))
        result.append(lax.ppermute(message, ("mid", "gy"), perm))
    return result


def level_kernel(potential_ref, level_ref):
    potential = jnp.concatenate(
        [potential_ref[:, at, :] for at in range(potential_ref.shape[1])], axis=1
    )
    level_ref[...] = level_rows(potential, level_ref.shape[0])


def split_kernel(bricks_y, cells_ref, level_ref, *refs):
    sent_refs, block_ref = refs[:-1], refs[-1]
    mid, y = lax.axis_index("mid"), lax.axis_index("gy")
    columns, plane = block_ref.shape
    share = columns // len(sent_refs)
    layers = cells_ref.shape[0] // plane
    extra = level_ref[...]
    for sent_ref in sent_refs:
        sent_ref[layers * share :, :] = extra
    for layer in range(layers):
        block = cells_ref[layer * plane : (layer + 1) * plane, :].astype(jnp.float32)
        block_ref[...] = block.T
        for step, sent_ref in zip(offsets(bricks_y), sent_refs):
            to_mid, to_y = ahead(mid, y, step, bricks_y)
            first = pl.multiple_of((to_mid * bricks_y + to_y) * share, share)
            own = block_ref[pl.ds(first, share), :]
            sent_ref[layer * share : (layer + 1) * share, :] = own.astype(jnp.bfloat16)


def split_columns(cells, potential, bricks_y):
    count, columns = cells.shape
    layers = potential.shape[0]
    plane = count // layers
    parts = owned * bricks_y
    message = jax.ShapeDtypeStruct(
        (layers * (columns // parts) + level_room(layers), plane), jnp.bfloat16
    )
    level = pl.pallas_call(
        level_kernel,
        out_shape=jax.ShapeDtypeStruct((level_room(layers), plane), jnp.bfloat16),
        compiler_params=pltpu.CompilerParams(vmem_limit_bytes=vmem_limit),
    )(potential)
    return pl.pallas_call(
        functools.partial(split_kernel, bricks_y),
        out_shape=[message] * parts,
        scratch_shapes=[pltpu.VMEM((columns, plane), jnp.float32)],
        compiler_params=pltpu.CompilerParams(vmem_limit_bytes=vmem_limit),
    )(cells, level)


def place_kernel(bricks_y, *refs):
    parts = owned * bricks_y
    received_refs, results = refs[:parts], refs[parts:]
    edge_ref, inner_ref, edge_level_ref, inner_level_ref, own_ref, level_ref = results
    mid, y, core = lax.axis_index("mid"), lax.axis_index("gy"), lax.axis_index("core")
    rows = own_ref.shape[2]
    layers = level_ref.shape[2]
    for step, received_ref in zip(offsets(bricks_y), received_refs):
        at, b = behind(mid, y, step, bricks_y)
        own_ref[at, b] = received_ref[:rows]
        extra = received_ref[rows:].astype(jnp.float32)
        level = extra[:layers] + extra[layers : 2 * layers] + extra[2 * layers : 3 * layers]
        level_ref[at, b] = level
    edge_ref[...] = own_ref[core]
    inner_ref[...] = own_ref[1 - core]
    edge_level_ref[...] = level_ref[core]
    inner_level_ref[...] = level_ref[1 - core]


def place(received, layers, bricks_y):
    plane = received[0].shape[1]
    rows = received[0].shape[0] - level_room(layers)
    field = (bricks_y, rows, plane)
    level = (bricks_y, layers, plane)
    return pl.pallas_call(
        functools.partial(place_kernel, bricks_y),
        out_shape=[jax.ShapeDtypeStruct(field, jnp.bfloat16)] * 2
        + [jax.ShapeDtypeStruct(level, jnp.float32)] * 2,
        scratch_shapes=[
            pltpu.VMEM((owned,) + field, jnp.bfloat16),
            pltpu.VMEM((owned,) + level, jnp.float32),
        ],
        compiler_params=pltpu.CompilerParams(vmem_limit_bytes=vmem_limit),
    )(*received)


def plane_kernel(own_ref, level_ref, weights_ref, partial_ref):
    bricks_y, rows, plane = own_ref.shape
    layers = level_ref.shape[1]
    share = rows // layers
    for b in range(bricks_y):
        fields, weights = [], []
        for kind, other in ((0, b), (1, b - 1), (2, b + 1)):
            if 0 <= other < bricks_y:
                for part in range(weights_ref.shape[1]):
                    fields.append(own_ref[other])
                    weights.append(weights_ref[kind, part])
        sides = jnp.dot(
            jnp.concatenate(fields, axis=1),
            jnp.concatenate(weights, axis=0),
            preferred_element_type=jnp.float32,
        )
        for layer in range(layers):
            here = slice(layer * share, (layer + 1) * share)
            level = jnp.broadcast_to(level_ref[b, layer : layer + 1, :], (share, plane))
            partial_ref[b, here] = sides[here] + level * own_ref[b, here].astype(jnp.float32)


def plane_part(own, level, weights):
    bricks_y, rows, plane = own.shape
    flops = 2 * bricks_y * bricks_y * 3 * rows * plane * plane
    return pl.pallas_call(
        plane_kernel,
        out_shape=jax.ShapeDtypeStruct(own.shape, jnp.float32),
        cost_estimate=pl.CostEstimate(flops=flops, bytes_accessed=own.size * 6, transcendentals=0),
        compiler_params=pltpu.CompilerParams(vmem_limit_bytes=vmem_limit),
    )(own, level, weights)


def layer_kernel(first, layers, pack, partial_ref, own_ref, outer_ref, other_ref, *refs):
    refs = list(refs)
    before_ref = None if first else refs.pop(0)
    inner_ref = refs.pop(0) if pack else None
    next_ref = refs.pop()
    core, mid, y = lax.axis_index("core"), lax.axis_index("mid"), lax.axis_index("gy")
    bricks_y, rows, plane = own_ref.shape
    share = rows // layers
    width = min(plane, 128)

    def step(low_ref, high_ref):
        for b in range(bricks_y):
            for column in range(0, share, group):
                for left in range(0, plane, width):
                    lane = slice(left, left + width)
                    places = [
                        slice(layer * share + column, layer * share + column + group)
                        for layer in range(layers)
                    ]
                    window = [
                        ref[b, here, lane].astype(jnp.float32)
                        for ref in (low_ref, own_ref, high_ref)
                        for here in places
                    ]
                    for layer, here in enumerate(places):
                        value = partial_ref[b, here, lane]
                        for distance in range(1, stencil_reach + 1):
                            pair = window[layers + layer - distance] + window[layers + layer + distance]
                            value = value + side_weights[distance] * pair
                        if before_ref is not None:
                            value = 2.0 * value - before_ref[b, here, lane].astype(jnp.float32)
                        next_ref[b, here, lane] = value.astype(jnp.bfloat16)

    @pl.when(core == 0)
    def _():
        step(outer_ref, other_ref)

    @pl.when(core != 0)
    def _():
        step(other_ref, outer_ref)

    if pack:
        for offset, sent_ref in zip(offsets(bricks_y), refs):
            to_mid, to_y = ahead(mid, y, offset, bricks_y)

            @pl.when(to_mid == core)
            def _():
                sent_ref[...] = next_ref[to_y]

            @pl.when(to_mid != core)
            def _():
                sent_ref[...] = inner_ref[to_y]


def layer_part(layers, partial, own, outer, other, before, inner=None):
    bricks_y, rows, plane = own.shape
    pack = inner is not None
    operands = [partial, own, outer, other]
    operands += [] if before is None else [before]
    operands += [inner] if pack else []
    one = jax.ShapeDtypeStruct((rows, plane), jnp.bfloat16)
    return pl.pallas_call(
        functools.partial(layer_kernel, before is None, layers, pack),
        out_shape=[one] * (owned * bricks_y) if pack else jax.ShapeDtypeStruct(own.shape, jnp.bfloat16),
        scratch_shapes=[pltpu.VMEM(own.shape, jnp.bfloat16)] if pack else [],
        cost_estimate=pl.CostEstimate(
            flops=24 * own.size, bytes_accessed=own.size * 14, transcendentals=0
        ),
        compiler_params=pltpu.CompilerParams(vmem_limit_bytes=vmem_limit),
    )(*operands)


def from_other_core(own):
    return lax.ppermute(own, "core", [(0, 1), (1, 0)])


def from_next_chip(edge):
    count = lax.axis_size(("far", "core"))
    pairs = [(at, at + 1) for at in range(1, count - 1, 2)]
    return lax.ppermute(edge, ("far", "core"), pairs + [(b, a) for a, b in pairs])


def chebyshev(edge, inner, edge_level, inner_level, weights):
    layers = edge_level.shape[1]
    edge_before = inner_before = None
    for stage in range(DEG):
        outer = from_next_chip(edge)
        other_inner = from_other_core(inner)
        other_edge = from_other_core(edge)
        edge_partial = plane_part(edge, edge_level, weights)
        inner_partial = plane_part(inner, inner_level, weights)
        inner_next = layer_part(layers, inner_partial, inner, other_inner, other_edge, inner_before)
        last = inner_next if stage == DEG - 1 else None
        edge_next = layer_part(layers, edge_partial, edge, outer, other_inner, edge_before, last)
        edge_before, edge = edge, edge_next
        inner_before, inner = inner, inner_next
    return edge


def join_kernel(bricks_y, *refs):
    parts = owned * bricks_y
    received_refs, (cells_ref, gram_ref, block_ref) = refs[:parts], refs[parts:]
    mid, y = lax.axis_index("mid"), lax.axis_index("gy")
    columns, plane = block_ref.shape
    share = columns // parts
    layers = cells_ref.shape[0] // plane
    total = None
    for layer in range(layers):
        for step, received_ref in zip(offsets(bricks_y), received_refs):
            from_mid, from_y = behind(mid, y, step, bricks_y)
            first = pl.multiple_of((from_mid * bricks_y + from_y) * share, share)
            own = received_ref[layer * share : (layer + 1) * share, :]
            block_ref[pl.ds(first, share), :] = own.astype(jnp.float32)
        block = block_ref[...]
        cells_ref[layer * plane : (layer + 1) * plane, :] = block.T.astype(jnp.bfloat16)
        narrow = block.astype(jnp.bfloat16)
        part = lax.dot_general(
            narrow, narrow, (((1,), (1,)), ((), ())), preferred_element_type=jnp.float32
        )
        total = part if total is None else total + part
    half = columns // 2
    packed = jnp.concatenate([total[:half], total[half:, half:]], axis=1)
    piece = gram_ref.shape[1]
    for device in range(gram_ref.shape[0]):
        gram_ref[device] = packed[device * piece : (device + 1) * piece]


def join_columns(received, layers, bricks_y):
    rows, plane = received[0].shape
    columns = rows // layers * owned * bricks_y
    half = columns // 2
    shares = math.gcd(lax.axis_size(axes), half)
    return pl.pallas_call(
        functools.partial(join_kernel, bricks_y),
        out_shape=(
            jax.ShapeDtypeStruct((layers * plane, columns), jnp.bfloat16),
            jax.ShapeDtypeStruct((shares, half // shares, 3 * half), jnp.float32),
        ),
        scratch_shapes=[pltpu.VMEM((columns, plane), jnp.float32)],
        compiler_params=pltpu.CompilerParams(vmem_limit_bytes=vmem_limit),
    )(*received)


lanes = 128
panel_rows = 8
block_rows = 64


def row_splat(values, row):
    return jnp.broadcast_to(values[row : row + 1, :], values.shape)


def lane_splat(values, lane):
    return jnp.broadcast_to(values[:, lane : lane + 1], (panel_rows, lanes))


def panel_inverse(columns):
    row = lax.broadcasted_iota(jnp.int32, (panel_rows, lanes), 0)
    columns = list(columns)
    full = [jnp.where(row == k, 1.0, 0.0).astype(jnp.float32) for k in range(panel_rows)]
    forward = list(full)
    scales = jnp.zeros((panel_rows, lanes), jnp.float32)
    for step in range(panel_rows):
        scale = 1.0 / row_splat(columns[step], step)
        scales = jnp.where(row == step, scale, scales)
        others = jnp.where(row == step, 0.0, columns[step])
        for k in range(step + 1, panel_rows):
            columns[k] = columns[k] - others * (row_splat(columns[k], step) * scale)
        for k in range(step):
            forward[k] = jnp.where(row == step, full[k], forward[k])
            full[k] = full[k] - others * (row_splat(full[k], step) * scale)
        full[step] = full[step] - others * scale
    root = jnp.sqrt(scales)
    full = [column * scales for column in full]
    forward = [column * root for column in forward]
    return full, forward


def combine(columns, rows):
    parts = []
    for left in range(0, rows.shape[1], lanes):
        piece = rows[:, left : left + lanes]
        terms = [column * row_splat(piece, k) for k, column in enumerate(columns)]
        while len(terms) > 1:
            terms = [a + b for a, b in zip(terms[::2], terms[1::2])]
        parts.append(terms[0])
    return jnp.concatenate(parts, axis=1)


def factor_kernel(scale, gram_ref, rows_ref, rotated_ref, upper_ref, packed_ref, factor_ref, inverse_ref):
    shares, piece, width = gram_ref.shape
    half = shares * piece
    order = 2 * half
    for share in range(shares):
        packed_ref[share * piece : (share + 1) * piece, :] = gram_ref[share]
    factor_ref[...] = jnp.zeros((order, order), jnp.float32)
    inverse_ref[...] = jnp.zeros((order, order), jnp.float32)
    for start in range(0, order, block_rows):
        left = start // lanes * lanes
        right = left + lanes
        local = start - left
        row = lax.broadcasted_iota(jnp.int32, (block_rows, right), 0)
        col = lax.broadcasted_iota(jnp.int32, (block_rows, right), 1)
        unit = jnp.where(col == row + start, 1.0, 0.0).astype(jnp.float32)
        at, side = (start, 0) if start < half else (start - half, order)
        own = packed_ref[at : at + block_rows, side : side + order - left]
        block = jnp.concatenate([own, unit], axis=1)
        if start > 0:
            done = jnp.concatenate(
                [factor_ref[:start, left:order], inverse_ref[:start, :right]], axis=1
            )
            update = lax.dot_general(
                factor_ref[:start, left : left + lanes],
                done,
                (((0,), (0,)), ((), ())),
                precision=lax.Precision.HIGHEST,
                preferred_element_type=jnp.float32,
            )
            block = block - update[local : local + block_rows]
        groups = [
            block[g : g + panel_rows] for g in range(0, block_rows, panel_rows)
        ]
        for index in range(len(groups)):
            lane = local + index * panel_rows
            rows = groups[index]
            full, forward = panel_inverse([lane_splat(rows, lane + k) for k in range(panel_rows)])
            step_rows = combine(full, rows)
            for other in range(index + 1, len(groups)):
                target = groups[other]
                columns = [lane_splat(target, lane + k) for k in range(panel_rows)]
                groups[other] = target - combine(columns, step_rows)
            finished = combine(forward, rows)
            at = start + index * panel_rows
            factor_ref[at : at + panel_rows, left:order] = finished[:, : order - left]
            inverse_ref[at : at + panel_rows, :right] = finished[:, order - left :]
    row = lax.broadcasted_iota(jnp.int32, (order, order), 0)
    col = lax.broadcasted_iota(jnp.int32, (order, order), 1)
    upper_ref[...] = jnp.where(col >= row, factor_ref[...] * (1.0 / scale), 0.0)
    inverse = jnp.where(col <= row, inverse_ref[...] * scale, 0.0)
    high = inverse.astype(jnp.bfloat16)
    rest = inverse - high.astype(jnp.float32)
    middle = rest.astype(jnp.bfloat16)
    low = (rest - middle.astype(jnp.float32)).astype(jnp.bfloat16)
    count = rows_ref.shape[0]
    chunk = math.gcd(count, 512)
    for at in range(0, count, chunk):
        piece = rows_ref[at : at + chunk, :]
        total = jnp.zeros((chunk, order), jnp.float32)
        for part in (low, middle, high):
            total = total + lax.dot_general(
                piece, part, (((1,), (1,)), ((), ())), preferred_element_type=jnp.float32
            )
        rotated_ref[at : at + chunk, :] = total.astype(jnp.bfloat16)


def factor_and_rotate(gram_matrix, rows, total_cells):
    order = rows.shape[1]
    count = rows.shape[0]
    return pl.pallas_call(
        functools.partial(factor_kernel, math.sqrt(total_cells)),
        out_shape=(
            jax.ShapeDtypeStruct((count, order), jnp.bfloat16),
            jax.ShapeDtypeStruct((order, order), jnp.float32),
        ),
        scratch_shapes=[
            pltpu.VMEM((order // 2, order // 2 * 3), jnp.float32),
            pltpu.VMEM((order, order), jnp.float32),
            pltpu.VMEM((order, order), jnp.float32),
        ],
        compiler_params=pltpu.CompilerParams(vmem_limit_bytes=vmem_limit),
    )(gram_matrix, rows)


def sum_over_devices(values):
    if lax.axis_size(axes) != values.shape[0]:
        return lax.psum(values, axes)
    total = jnp.sum(lax.all_to_all(values, axes, 0, 0), axis=0)
    return lax.all_to_all(jnp.broadcast_to(total[None], values.shape), axes, 0, 0)


def shards(trial_orbitals, potential):
    layers, extent_y, extent_z, columns = trial_orbitals.shape
    bricks_y = lax.axis_size("gy")
    total_cells = lax.axis_size(axes) * layers * extent_y * extent_z
    weights = jnp.asarray(plane_weights(extent_y, extent_z))

    cells = trial_orbitals.reshape(layers * extent_y * extent_z, columns)
    sent = split_columns(cells, potential, bricks_y)
    placed = place(exchange(sent, bricks_y), layers, bricks_y)
    sent = chebyshev(*placed, weights)
    rows, local_gram = join_columns(exchange(sent, bricks_y), layers, bricks_y)
    gram_matrix = sum_over_devices(local_gram)
    rotated, upper_factor = factor_and_rotate(gram_matrix, rows, total_cells)
    return (rotated.reshape(trial_orbitals.shape), upper_factor)


def solution(mesh):
    bricks_x, bricks_y = mesh.devices.shape
    cut = Mesh(mesh.devices.reshape(bricks_x // 4, owned, 2, bricks_y), axes)
    cells = P(("far", "mid", "core"), "gy")
    return jax.shard_map(
        shards,
        mesh=cut,
        in_specs=(cells, cells),
        out_specs=(cells, P()),
        check_vma=False,
    )
```
